512 devices in a mesh: chan: 64 (over z_lo, x, core), freq: 8 (over y, z_hi).
Axes of the slice: x: 4, y: 4, z: 16 (z_hi: 2, z_lo: 8; z = z_hi * 8 + z_lo), core: 2. Of those that a mesh axis runs over, the one named last changes fastest.
Arguments:
- spectra: bfloat16 [20, 272, 2, 8192], P(None, 'freq', None, 'chan'), may hold values from -18 to 18
- valid: int32 [20, 8192], P(None, 'chan'), may hold values from 0 to 1
Outputs:
- correlation: float32 [4, 64, 51, 128, 128], P(None, 'chan', None, 'freq')
The draws below stay inside these ranges and needn't reach their ends.
All inputs are finite; a program needn't handle non-finite values.
Results may differ from the reference program's by a relative error of at most 0.0045.
Values may be sent and summed in bfloat16 or wider, within the bound.
A program may use at most 64 MiB of HBM per device.

```python
import math
import jax
import jax.numpy as jnp
from jax import lax

W = 20
BINS = 272
CH = 128
LAGS = 51
ROUNDS = 4
SMOOTH = 4
BLOCKS = 64
CHANNELS = 8192


def draw_spectra(key, part):
    key = jax.random.fold_in(key, 11)
    key_scale, key_values = jax.random.split(key, 2)
    channel_scale = jnp.exp(jax.random.uniform(key_scale, (CHANNELS,), jnp.float32, math.log(0.1), math.log(3.0)))
    values = jnp.clip(jax.random.normal(key_values, (W, BINS, 2, CHANNELS), jnp.float32), -6.0, 6.0)
    return (values * channel_scale).astype(jnp.bfloat16)


def draw_valid(key, part):
    key = jax.random.fold_in(key, 23)
    key_dead, key_live = jax.random.split(key, 2)
    dead_trace = jax.random.randint(key_dead, (CHANNELS,), 0, 16) == 0
    live_window = jax.random.randint(key_live, (W, CHANNELS), 0, 5) != 0
    return jnp.where(live_window & jnp.logical_not(dead_trace)[None, :], 1, 0).astype(jnp.int32)


def setup_inputs(seed: int = 0) -> dict:
    splits = jax.random.split(jax.random.key(seed), 3)
    return {
        "spectra": draw_spectra(jax.random.fold_in(splits[2], 71), 0),
        "valid": draw_valid(jax.random.fold_in(splits[2], 71), 0),
    }


water_level = 0.5
first_bin = 30.0
period = 600.0

def whiten(block_spectra, block_valid):
    values = block_spectra.astype(jnp.float32)
    magnitude = jnp.sqrt(values[:, :, 0] * values[:, :, 0] + values[:, :, 1] * values[:, :, 1])
    padded = jnp.pad(magnitude, ((0, 0), (SMOOTH, SMOOTH), (0, 0)))
    running_sum = padded[:, 0:BINS]
    for offset in range(1, 2 * SMOOTH + 1):
        running_sum = running_sum + padded[:, offset:offset + BINS]
    bin_index = jnp.arange(BINS, dtype=jnp.int32)
    bin_count = (jnp.minimum(bin_index + SMOOTH, BINS - 1) - jnp.maximum(bin_index - SMOOTH, 0) + 1).astype(jnp.float32)
    water_mark = jnp.maximum(running_sum / bin_count[None, :, None], water_level)
    factor = block_valid.astype(jnp.float32)[:, None, :] / water_mark
    return (values * factor[:, :, None, :]).astype(jnp.bfloat16)

def make_table():
    lag_index = jnp.arange(LAGS, dtype=jnp.float32) - float(LAGS // 2)
    bin_freq = first_bin + jnp.arange(BINS, dtype=jnp.float32)
    phase_angle = 2.0 * math.pi * lag_index[:, None] * bin_freq[None, :] / period
    return jnp.concatenate([jnp.cos(phase_angle), -jnp.sin(phase_angle)], axis=1).astype(jnp.bfloat16)

def pair_lags(own_block, partner_block, own_valid, partner_valid, lag_table):
    rotated = jnp.stack([partner_block[:, :, 1], -partner_block[:, :, 0]], axis=2)
    both_parts = jnp.concatenate([partner_block, rotated], axis=3)
    cross = jnp.einsum('wfpa,wfpb->fab', own_block.astype(jnp.float32), both_parts.astype(jnp.float32))
    pairs = jnp.dot(own_valid.astype(jnp.float32).T, partner_valid.astype(jnp.float32))
    divisor = jnp.maximum(jnp.concatenate([pairs, pairs], axis=1), 1.0)
    stacked = (cross / divisor[None]).astype(jnp.bfloat16)
    combined = jnp.concatenate([stacked[:, :, :CH], stacked[:, :, CH:]], axis=0)
    lag_values = jnp.dot(lag_table, combined.reshape(2 * BINS, CH * CH), preferred_element_type=jnp.float32)
    return lag_values.reshape(LAGS, CH, CH)

def reference(spectra, valid):
    blocks = jnp.transpose(spectra.reshape(W, BINS, 2, BLOCKS, CH), (3, 0, 1, 2, 4))
    block_valid = jnp.transpose(valid.reshape(W, BLOCKS, CH), (1, 0, 2))

    def whiten_one(pieces):
        return whiten(pieces[0], pieces[1])
    whitened = lax.map(whiten_one, (blocks, block_valid))
    lag_table = make_table()
    results = []
    for round_index in range(ROUNDS):
        partners = jnp.roll(whitened, round_index, axis=0)
        partner_valid = jnp.roll(block_valid, round_index, axis=0)

        def one_pair(pieces):
            return pair_lags(pieces[0], pieces[1], pieces[2], pieces[3], lag_table)
        results.append(lax.map(one_pair, (whitened, partners, block_valid, partner_valid)))
    return jnp.stack(results, axis=0)
```

```python
import functools
import math

import jax
import jax.numpy as jnp
from jax import lax
from jax.experimental import pallas as pl
from jax.experimental.pallas import tpu as pltpu
from jax.sharding import PartitionSpec as P

W = 20
BINS = 272
CH = 128
LAGS = 51
ROUNDS = 4
SMOOTH = 4
BLOCKS = 64

BAND = 34
GROUP = 68
ROWS = 2 * W
PAIR = 2 * ROWS
HALO = SMOOTH * ROWS
BAND_ROWS = BAND * ROWS
GROUP_ROWS = GROUP * ROWS
FLAG_ROWS = 48
STRIDE = 2 * GROUP
LAG_PAD = 56
OWN_ROWS = 16
HALF = 64
EDGES = ((0, 4), (30, 4))
MIDDLE = ((4, 12), (16, 10), (26, 4))
WHITEN = ((0, 6), (6, 5), (11, 6))

water_level = 0.5
first_bin = 30.0
period = 600.0
MESH = pl.DeviceIdType.MESH


def make_table():
    lag_index = jnp.arange(LAGS, dtype=jnp.float32) - float(LAGS // 2)
    bin_freq = first_bin + jnp.arange(BINS, dtype=jnp.float32)
    phase_angle = 2.0 * math.pi * lag_index[:, None] * bin_freq[None, :] / period
    return jnp.stack([jnp.cos(phase_angle), -jnp.sin(phase_angle)], axis=1).astype(jnp.bfloat16)


def roll4(x):
    return pltpu.roll(x, 4, axis=1)


def kernel(
    raw, flags, table, out,
    band, mag, white, lhs, inverse, spread, lagged, outbox, inbox,
    load_sem, z_send, z_recv, h_send, h_recv, f_send, f_recv, x_send, x_recv, y_send, y_recv,
):
    i, j = lax.axis_index("chan"), lax.axis_index("freq")
    y, zhi = j // 2, j % 2
    core = i % 2
    other = 1 - zhi

    def ahead(r):
        t = i + r + BLOCKS
        flip = (t // BLOCKS + 1) % 2
        return {"chan": t % BLOCKS, "freq": j + flip * (1 - 2 * zhi)}

    def along_y(d):
        return {"chan": i, "freq": ((y + d) % 4) * 2 + zhi}

    across = {"chan": i, "freq": j + 1 - 2 * zhi}
    own_at = HALO + zhi * BAND_ROWS
    other_at = HALO + other * BAND_ROWS

    def remote(src, dst, send, recv, device):
        return pltpu.make_async_remote_copy(
            src_ref=src, dst_ref=dst, send_sem=send, recv_sem=recv,
            device_id=device, device_id_type=MESH,
        )

    load = pltpu.make_async_copy(raw, band.at[pl.ds(own_at, BAND_ROWS)], load_sem)
    load.start()
    barrier = pltpu.get_barrier_semaphore()
    partners = [across] + [along_y(d) for d in (1, 2, 3)]
    partners += [ahead(r) for r in (1, 2, 3, -1, -2, -3)]
    for partner in partners:
        pl.semaphore_signal(barrier, inc=1, device_id=partner, device_id_type=MESH)
    white[0, 0:FLAG_ROWS, :] = flags[...].astype(jnp.bfloat16)
    load.wait()
    pl.semaphore_wait(barrier, len(partners))

    z_pieces = EDGES + MIDDLE

    def z_copy(k):
        first, bins = z_pieces[k]
        here = band.at[pl.ds(own_at + first * ROWS, bins * ROWS)]
        return remote(here, here, z_send.at[k], z_recv.at[k], across)

    for k in range(len(z_pieces)):
        z_copy(k).start()

    def halo_copy(top, k):
        src = HALO + GROUP_ROWS - HALO if top else HALO
        dst = 0 if top else HALO + GROUP_ROWS
        return remote(
            band.at[pl.ds(src, HALO)], band.at[pl.ds(dst, HALO)],
            h_send.at[k], h_recv.at[k], along_y(1 if top else 3),
        )

    @pl.when(zhi == 1)
    def _():
        halo_copy(True, 0).start()

    @pl.when(zhi == 0)
    def _():
        halo_copy(False, 1).start()

    flag_copies = [
        remote(
            white.at[0, pl.ds(0, FLAG_ROWS)], white.at[r, pl.ds(0, FLAG_ROWS)],
            f_send.at[r - 1], f_recv.at[r - 1], ahead(r),
        )
        for r in (1, 2, 3)
    ]
    for copy in flag_copies:
        copy.start()

    sublane = lax.broadcasted_iota(jnp.int32, (1, 8, CH), 1)
    lane = lax.broadcasted_iota(jnp.int32, (1, 8, CH), 2)
    sign = jnp.where(sublane < 4, -1.0, 1.0)
    first_half = (lane % 32) < 16
    valid = flags[0:ROWS, :].astype(jnp.float32)

    def magnitudes(row, pairs):
        def body(p, carry):
            at = pl.multiple_of(row + p * PAIR, 16)
            v = band[pl.ds(at, PAIR), :].astype(jnp.float32).reshape(10, 8, CH)
            square = v * v
            m = jnp.sqrt(square + roll4(square))
            mag[pl.ds(at, PAIR), :] = m.reshape(PAIR, CH)
            return carry

        lax.fori_loop(0, pairs, body, 0, unroll=2 if pairs % 2 == 0 else 1)

    def whiten(first_pair, pairs):
        def body(p, carry):
            pair = first_pair + p
            row = pl.multiple_of(pair * PAIR, 16)
            m = [mag[pl.ds(pl.multiple_of(row + t * ROWS, 8), ROWS), :] for t in range(10)]
            inner = ((m[1] + m[2]) + (m[3] + m[4])) + ((m[5] + m[6]) + (m[7] + m[8]))
            outs = []
            for t in range(2):
                bin_index = y * GROUP + 2 * pair + t
                count = (
                    jnp.minimum(bin_index + SMOOTH, BINS - 1) - jnp.maximum(bin_index - SMOOTH, 0) + 1
                ).astype(jnp.float32)
                total = inner + (m[0] if t == 0 else m[9])
                water = jnp.maximum(total / jnp.full((ROWS, CH), count, jnp.float32), water_level)
                outs.append(valid / water)
            factor = jnp.concatenate(outs, axis=0)
            v = band[pl.ds(pl.multiple_of(row + HALO, 16), PAIR), :].astype(jnp.float32)
            w = (v * factor).astype(jnp.bfloat16)
            white[0, pl.ds(pl.multiple_of(FLAG_ROWS + row, 16), PAIR), :] = w
            a1 = pltpu.roll(w.astype(jnp.float32).reshape(10, 8, CH), 112 * zhi, axis=2)
            a2 = pltpu.roll(roll4(a1) * sign, 16, axis=2)
            both = jnp.where(first_half, a1, a2).reshape(PAIR, CH)
            turned = jnp.transpose(both)
            column = lax.broadcasted_iota(jnp.int32, (CH, PAIR), 1)
            lhs[pair, 0:CH, 0:PAIR] = jnp.where(column < ROWS, turned, 0.0).astype(jnp.bfloat16)
            lhs[pair, CH : 2 * CH, 0:PAIR] = jnp.where(column < ROWS, 0.0, turned).astype(jnp.bfloat16)
            return carry

        lax.fori_loop(0, pairs, body, 0)

    def cross(r, first_pair, pairs):
        def body(p, carry):
            pair = first_pair + p
            rhs = white[r, pl.ds(pl.multiple_of(FLAG_ROWS + pair * PAIR, 16), PAIR), :]
            c = jnp.dot(lhs[pair, :, 0:PAIR], rhs, preferred_element_type=jnp.float32)
            for t in range(2):
                for g in range(4):
                    scale = inverse[r, g * 16 : (g + 1) * 16, :]
                    for part in range(2):
                        at = t * CH + g * 32 + part * 16
                        start = g * 16 * STRIDE + part * GROUP + 2 * pair + t
                        spread[pl.ds(start, 16, stride=STRIDE), :] = c[at : at + 16, :] * scale
            return carry

        lax.fori_loop(0, pairs, body, 0)

    def usable_pairs(r):
        mine = white[0, 0:FLAG_ROWS, :].astype(jnp.float32)
        mine = pltpu.roll(mine, 112 * zhi, axis=1)
        n = jnp.dot(
            jnp.transpose(mine).astype(jnp.bfloat16), white[r, 0:FLAG_ROWS, :],
            preferred_element_type=jnp.float32,
        )
        scale = 1.0 / jnp.maximum(n * 0.5, 1.0)
        for g in range(4):
            inverse[r, g * 16 : (g + 1) * 16, :] = scale[g * 32 : g * 32 + 16, :]

    def lags(r):
        tab = table[...]

        def body(p, carry):
            a = 2 * p
            s0 = spread[pl.ds(pl.multiple_of(a * STRIDE, 8), STRIDE), :].astype(jnp.bfloat16)
            s1 = spread[pl.ds(pl.multiple_of((a + 1) * STRIDE, 8), STRIDE), :].astype(jnp.bfloat16)
            both = jnp.concatenate([s0, s1], axis=1)
            c = jnp.dot(tab, both, preferred_element_type=jnp.float32)
            lagged[r, pl.ds(a, LAG_PAD, stride=HALF), :] = c[:, 0:CH]
            lagged[r, pl.ds(a + 1, LAG_PAD, stride=HALF), :] = c[:, CH : 2 * CH]
            return carry

        lax.fori_loop(0, HALF // 2, body, 0)

        for d in (2, 1, 3):
            to = (y + d) % 4

            def pack(l, carry):
                at = pl.multiple_of(l * HALF + to * OWN_ROWS, 16)
                outbox[r, d - 1, pl.ds(pl.multiple_of(l * OWN_ROWS, 16), OWN_ROWS), :] = lagged[
                    r, pl.ds(at, OWN_ROWS), :
                ].astype(jnp.bfloat16)
                return carry

            lax.fori_loop(0, LAGS, pack, 0, unroll=3)
            y_copy(r, d).start()

    def y_copy(r, d):
        return remote(
            outbox.at[r, d - 1], inbox.at[r, d - 1], y_send.at[r, d - 1], y_recv.at[r, d - 1], along_y(d)
        )

    def piece(slot, k, origin):
        if k == 0:
            return white.at[slot, pl.ds(FLAG_ROWS + origin * BAND_ROWS, BAND_ROWS)]
        first, pairs = WHITEN[k - 1]
        return white.at[slot, pl.ds(FLAG_ROWS + (1 - origin) * BAND_ROWS + first * PAIR, pairs * PAIR)]

    x_index = (i // 2) % 4
    z_index = zhi * 8 + i // 8
    before = jnp.where(x_index == 0, ((z_index + 15) % 16) // 8, zhi)

    def to_sibling(k):
        return remote(piece(0, k, zhi), piece(1, k, zhi), x_send.at[0, k], x_recv.at[0, k], ahead(1))

    def to_next(k):
        return remote(piece(0, k, zhi), piece(2, k, zhi), x_send.at[1, k], x_recv.at[1, k], ahead(2))

    def pass_up(k):
        return remote(piece(2, k, before), piece(3, k, before), x_send.at[2, k], x_recv.at[2, k], ahead(1))

    def pass_down(k):
        return remote(piece(2, k, before), piece(1, k, before), x_send.at[2, k], x_recv.at[0, k], ahead(-1))

    def pass_on(k):
        return remote(piece(2, k, before), piece(3, k, before), x_send.at[0, k], x_recv.at[2, k], ahead(1))

    def send_own(k):
        to_next(k).start()

        @pl.when(core == 0)
        def _():
            to_sibling(k).start()

    def forward(k):
        to_next(k).wait_recv()

        @pl.when(core == 0)
        def _():
            pass_up(k).start()

        @pl.when(core == 1)
        def _():
            pass_down(k).start()
            pass_on(k).start()

    magnitudes(own_at, BAND // 2)
    usable_pairs(0)
    for k in range(len(EDGES)):
        z_copy(k).wait_recv()

    @pl.when(zhi == 0)
    def _():
        halo_copy(True, 0).start()

    @pl.when(zhi == 1)
    def _():
        halo_copy(False, 1).start()

    for first, bins in EDGES:
        magnitudes(other_at + first * ROWS, bins // 2)
    halo_copy(True, 0).wait_recv()
    halo_copy(False, 1).wait_recv()
    magnitudes(0, SMOOTH // 2)
    magnitudes(HALO + GROUP_ROWS, SMOOTH // 2)

    @pl.when(y == 0)
    def _():
        mag[0:HALO, :] = jnp.zeros((HALO, CH), jnp.float32)

    @pl.when(y == 3)
    def _():
        mag[HALO + GROUP_ROWS :, :] = jnp.zeros((HALO, CH), jnp.float32)

    whiten(zhi * (BAND // 2), BAND // 2)
    send_own(0)
    cross(0, zhi * (BAND // 2), BAND // 2)
    for k in (1, 2, 3):
        z_copy(1 + k).wait_recv()
        first, bins = MIDDLE[k - 1]
        magnitudes(other_at + first * ROWS, bins // 2)
        first, pairs = WHITEN[k - 1]
        whiten(other * (BAND // 2) + first, pairs)
        send_own(k)
        forward(k - 1)
        cross(0, other * (BAND // 2) + first, pairs)
    forward(3)
    lags(0)
    for r in (1, 2, 3):
        flag_copies[r - 1].wait_recv()
        usable_pairs(r)
        if r != 2:
            for k in range(4):
                remote(
                    piece(r, k, zhi), piece(r, k, zhi), x_send.at[0, k], x_recv.at[r - 1, k], ahead(1)
                ).wait_recv()
        cross(r, 0, GROUP // 2)
        lags(r)

    for r in range(ROUNDS):
        for d in (1, 2, 3):
            y_copy(r, d).wait_recv()

        def total(l, carry):
            at = pl.multiple_of(l * OWN_ROWS, 16)
            mine = lagged[r, pl.ds(pl.multiple_of(l * HALF + y * OWN_ROWS, 16), OWN_ROWS), :]
            got = [inbox[r, d, pl.ds(at, OWN_ROWS), :].astype(jnp.float32) for d in range(3)]
            out[r, pl.ds(at, OWN_ROWS), :] = (mine + got[0]) + (got[1] + got[2])
            return carry

        lax.fori_loop(0, LAGS, total, 0, unroll=3)

    for k in range(len(z_pieces)):
        z_copy(k).wait_send()
    halo_copy(True, 0).wait_send()
    halo_copy(False, 1).wait_send()
    for copy in flag_copies:
        copy.wait_send()
    for k in range(4):
        to_next(k).wait_send()
        to_sibling(k).wait_send()
        pass_up(k).wait_send()
    for r in range(ROUNDS):
        for d in (1, 2, 3):
            y_copy(r, d).wait_send()


def on_device(spectra, valid):
    groups = spectra.reshape(5, 4, BAND, 2, CH)
    raw = jnp.transpose(groups, (2, 0, 3, 1, 4)).reshape(BAND_ROWS, CH)
    flags = valid.astype(jnp.float32).reshape(5, 1, 4, CH)
    flags = jnp.broadcast_to(flags, (5, 2, 4, CH)).reshape(ROWS, CH)
    flags = jnp.pad(flags, ((0, FLAG_ROWS - ROWS), (0, 0)))
    y = lax.axis_index("freq") // 2
    table = lax.dynamic_slice_in_dim(make_table(), y * GROUP, GROUP, axis=2)
    table = jnp.pad(table.reshape(LAGS, STRIDE), ((0, LAG_PAD - LAGS), (0, 0)))
    vmem = pl.BlockSpec(memory_space=pltpu.VMEM)
    dma = pltpu.SemaphoreType.DMA
    bf16, f32 = jnp.bfloat16, jnp.float32
    out = pl.pallas_call(
        kernel,
        out_shape=jax.ShapeDtypeStruct((ROUNDS, LAGS * OWN_ROWS, CH), f32),
        in_specs=[pl.BlockSpec(memory_space=pl.ANY), vmem, vmem],
        out_specs=vmem,
        scratch_shapes=[
            pltpu.VMEM((GROUP_ROWS + 2 * HALO, CH), bf16),
            pltpu.VMEM((GROUP_ROWS + 2 * HALO, CH), f32),
            pltpu.VMEM((ROUNDS, FLAG_ROWS + GROUP_ROWS, CH), bf16),
            pltpu.VMEM((GROUP // 2, 2 * CH, CH), bf16),
            pltpu.VMEM((ROUNDS, HALF, CH), f32),
            pltpu.VMEM((HALF * STRIDE, CH), f32),
            pltpu.VMEM((ROUNDS, LAG_PAD * HALF, CH), f32),
            pltpu.VMEM((ROUNDS, 3, LAGS * OWN_ROWS, CH), bf16),
            pltpu.VMEM((ROUNDS, 3, LAGS * OWN_ROWS, CH), bf16),
            dma, dma((5,)), dma((5,)), dma((2,)), dma((2,)), dma((3,)), dma((3,)),
            dma((3, 4)), dma((3, 4)), dma((4, 3)), dma((4, 3)),
        ],
        compiler_params=pltpu.CompilerParams(
            collective_id=0, has_side_effects=True, vmem_limit_bytes=48 << 20
        ),
        name="correlate",
    )(raw, flags, table)
    return out.reshape(ROUNDS, 1, LAGS, OWN_ROWS, CH)


def solution(mesh):
    return jax.shard_map(
        on_device,
        mesh=mesh,
        in_specs=(P(None, "freq", None, "chan"), P(None, "chan")),
        out_specs=P(None, "chan", None, "freq", None),
        check_vma=False,
    )
```

```python
import math

import jax
import jax.numpy as jnp
import numpy as np
from jax import lax
from jax.experimental import pallas as pl
from jax.experimental.pallas import tpu as pltpu
from jax.sharding import PartitionSpec as P

W = 20
BINS = 272
CH = 128
LAGS = 51
ROUNDS = 4
SMOOTH = 4
BLOCKS = 64

BAND = 34
GROUP = 68
PAIRS = GROUP // 2
ROWS = 2 * W
PAIR = 2 * ROWS
HALO = SMOOTH * ROWS
BAND_ROWS = BAND * ROWS
GROUP_ROWS = GROUP * ROWS
FLAG_ROWS = 48
STRIDE = 2 * GROUP
LAG_STORE = 56
LAG_PAD = 64
OWN_ROWS = 16
HALF = 64
CUT = 26 * OWN_ROWS
FULL = LAGS * OWN_ROWS
ACROSS = ((0, 2), (12, 5), (8, 4), (4, 4), (2, 2))
WHITEN = ((2, 13), (0, 2), (15, 5), (20, 4), (24, 4), (28, 6))
PIECES = len(WHITEN)

water_level = 0.5
first_bin = 30.0
period = 600.0
MESH = pl.DeviceIdType.MESH


def make_table():
    lag_index = np.arange(LAGS, dtype=np.float32) - np.float32(LAGS // 2)
    bin_freq = np.float32(first_bin) + np.arange(BINS, dtype=np.float32)
    phase = np.float32(2.0 * math.pi) * lag_index[:, None] * bin_freq[None, :] / np.float32(period)
    both = np.stack([np.cos(phase), -np.sin(phase)], axis=1).reshape(LAGS, 2, 4, GROUP)
    table = np.zeros((4, LAG_PAD, 2, GROUP), np.float32)
    table[:, :LAGS] = both.transpose(2, 0, 1, 3)
    return jnp.asarray(table.reshape(4, LAG_PAD, STRIDE), jnp.bfloat16)


def roll4(x):
    return pltpu.roll(x, 4, axis=1)


def loop(count, body):
    lax.fori_loop(0, count, lambda n, carry: (body(n), carry)[1], 0, unroll=unrolled(count))


def unrolled(count):
    return max(n for n in range(1, 18) if count % n == 0)


def kernel(
    raw, flags, table, out,
    band, mag, white, lhs, inverse, spread, lagged, outbox, inbox,
    load_sem, z_send, z_recv, h_send, h_recv, f_send, f_recv, x_send, x_recv, y_send, y_recv,
):
    i, j = lax.axis_index("chan"), lax.axis_index("freq")
    y, zhi = j // 2, j % 2
    core = i % 2
    x_index = (i // 2) % 4
    z_index = zhi * 8 + i // 8
    before = jnp.where(x_index == 0, ((z_index + 15) % 16) // 8, zhi)

    def ahead(r):
        t = i + r + BLOCKS
        flip = (t // BLOCKS + 1) % 2
        return {"chan": t % BLOCKS, "freq": j + flip * (1 - 2 * zhi)}

    def along_y(d):
        return {"chan": i, "freq": ((y + d) % 4) * 2 + zhi}

    across = {"chan": i, "freq": j + 1 - 2 * zhi}

    def first_pair(first, pairs, origin):
        return first + origin * (PAIRS - 2 * first - pairs)

    def remote(src, dst, send, recv, device):
        return pltpu.make_async_remote_copy(
            src_ref=src, dst_ref=dst, send_sem=send, recv_sem=recv,
            device_id=device, device_id_type=MESH,
        )

    load = pltpu.make_async_copy(raw, band.at[pl.ds(HALO + zhi * BAND_ROWS, BAND_ROWS)], load_sem)
    load.start()
    barrier = pltpu.get_barrier_semaphore()
    partners = [across] + [along_y(d) for d in (1, 3)]
    partners += [ahead(r) for r in (1, 2, 3, -1, -2, -3)]
    for partner in partners:
        pl.semaphore_signal(barrier, inc=1, device_id=partner, device_id_type=MESH)
    white[0, 0:FLAG_ROWS, :] = flags[...].astype(jnp.bfloat16)
    load.wait()
    pl.semaphore_wait(barrier, len(partners))

    def z_copy(k):
        first, pairs = ACROSS[k]
        here = band.at[pl.ds(HALO + first_pair(first, pairs, zhi) * PAIR, pairs * PAIR)]
        return remote(here, here, z_send.at[k], z_recv.at[k], across)

    def halo_copy(top):
        src = GROUP_ROWS if top else HALO
        dst = 0 if top else HALO + GROUP_ROWS
        k = 0 if top else 1
        return remote(
            band.at[pl.ds(src, HALO)], band.at[pl.ds(dst, HALO)],
            h_send.at[k], h_recv.at[k], along_y(1 if top else 3),
        )

    def send_halo(own):
        pl.when(zhi == own)(halo_copy(True).start)
        pl.when(zhi != own)(halo_copy(False).start)

    flag_copies = [
        remote(
            white.at[0, pl.ds(0, FLAG_ROWS)], white.at[r, pl.ds(0, FLAG_ROWS)],
            f_send.at[r - 1], f_recv.at[r - 1], ahead(r),
        )
        for r in (1, 2, 3)
    ]

    sublane = lax.broadcasted_iota(jnp.int32, (1, 8, CH), 1)
    lane = lax.broadcasted_iota(jnp.int32, (1, 8, CH), 2)
    sign = jnp.where(sublane < 4, -1.0, 1.0)
    first_half = (lane % 32) < 16
    valid = flags[0:ROWS, :]

    def magnitudes(row, pairs):
        def body(p):
            at = pl.multiple_of(row + p * PAIR, 16)
            v = band[pl.ds(at, PAIR), :].astype(jnp.float32).reshape(10, 8, CH)
            square = v * v
            m = jnp.sqrt(square + roll4(square))
            mag[pl.ds(at, PAIR), :] = m.reshape(PAIR, CH)

        loop(pairs, body)

    def whiten(start, pairs):
        def body(p):
            pair = start + p
            row = pl.multiple_of(pair * PAIR, 16)
            m = [mag[pl.ds(pl.multiple_of(row + t * ROWS, 8), ROWS), :] for t in range(10)]
            inner = ((m[1] + m[2]) + (m[3] + m[4])) + ((m[5] + m[6]) + (m[7] + m[8]))
            outs = []
            for t in range(2):
                bin_index = y * GROUP + 2 * pair + t
                count = (
                    jnp.minimum(bin_index + SMOOTH, BINS - 1) - jnp.maximum(bin_index - SMOOTH, 0) + 1
                ).astype(jnp.float32)
                total = inner + (m[0] if t == 0 else m[9])
                water = jnp.maximum(total / jnp.full((1, CH), count, jnp.float32), water_level)
                outs.append(valid / water)
            factor = jnp.concatenate(outs, axis=0)
            v = band[pl.ds(pl.multiple_of(row + HALO, 16), PAIR), :].astype(jnp.float32)
            w = (v * factor).astype(jnp.bfloat16)
            white[0, pl.ds(pl.multiple_of(FLAG_ROWS + row, 16), PAIR), :] = w
            a1 = pltpu.roll(w.astype(jnp.float32).reshape(10, 8, CH), 112 * zhi, axis=2)
            a2 = pltpu.roll(roll4(a1) * sign, 16, axis=2)
            both = jnp.where(first_half, a1, a2).reshape(PAIR, CH)
            turned = jnp.transpose(both)
            column = lax.broadcasted_iota(jnp.int32, (CH, PAIR), 1)
            lhs[pair, 0:CH, 0:PAIR] = jnp.where(column < ROWS, turned, 0.0).astype(jnp.bfloat16)
            lhs[pair, CH : 2 * CH, 0:PAIR] = jnp.where(column < ROWS, 0.0, turned).astype(jnp.bfloat16)

        loop(pairs, body)

    def cross(r, start, pairs):
        def body(p):
            pair = start + p
            rhs = white[r, pl.ds(pl.multiple_of(FLAG_ROWS + pair * PAIR, 16), PAIR), :]
            c = jnp.dot(lhs[pair, :, 0:PAIR], rhs, preferred_element_type=jnp.float32)
            for g in range(4):
                scale = inverse[r, g * 16 : (g + 1) * 16, :]
                for t in range(2):
                    for part in range(2):
                        at = t * CH + g * 32 + part * 16
                        row = g * 16 * STRIDE + part * GROUP + 2 * pair + t
                        spread[pl.ds(row, 16, stride=STRIDE), :] = c[at : at + 16, :] * scale

        loop(pairs, body)

    def usable_pairs(r):
        mine = white[0, 0:FLAG_ROWS, :].astype(jnp.float32)
        mine = pltpu.roll(mine, 112 * zhi, axis=1)
        n = jnp.dot(
            jnp.transpose(mine).astype(jnp.bfloat16), white[r, 0:FLAG_ROWS, :],
            preferred_element_type=jnp.float32,
        )
        scale = 1.0 / jnp.maximum(n * 0.5, 1.0)
        for g in range(4):
            inverse[r, g * 16 : (g + 1) * 16, :] = scale[g * 32 : g * 32 + 16, :]

    def lag_sums(r):
        tab = table[y]

        def body(p):
            a = 2 * p
            s0 = spread[pl.ds(pl.multiple_of(a * STRIDE, 8), STRIDE), :].astype(jnp.bfloat16)
            s1 = spread[pl.ds(pl.multiple_of((a + 1) * STRIDE, 8), STRIDE), :].astype(jnp.bfloat16)
            both = jnp.concatenate([s0, s1], axis=1)
            c = jnp.dot(tab, both, preferred_element_type=jnp.float32)
            lagged[r, pl.ds(a, LAG_STORE, stride=HALF), :] = c[0:LAG_STORE, 0:CH]
            lagged[r, pl.ds(a + 1, LAG_STORE, stride=HALF), :] = c[0:LAG_STORE, CH : 2 * CH]

        loop(HALF // 2, body)

    PARTS = ((2, 0, 1), (2, CUT, 3), (1, CUT, 1), (3, 0, 3), (1, 0, 1), (3, CUT, 3))

    def y_copy(r, n):
        d, row, way = PARTS[n]
        part = pl.ds(row, CUT if row == 0 else FULL - CUT)
        return remote(
            outbox.at[r, d - 1, part], inbox.at[r, d - 1, part], y_send.at[r, n], y_recv.at[r, n], along_y(way)
        )

    def pack_round(r, n):
        d, row, _ = PARTS[n]
        to = (y + d) % 4

        def body(l):
            at = pl.multiple_of(row + l * OWN_ROWS, 16)
            from_row = pl.multiple_of(row // OWN_ROWS * HALF + l * HALF + to * OWN_ROWS, 16)
            sums = lagged[r, pl.ds(from_row, OWN_ROWS), :]
            if n >= 4:
                sums = sums + inbox[r, 1, pl.ds(at, OWN_ROWS), :].astype(jnp.float32)
            outbox[r, d - 1, pl.ds(at, OWN_ROWS), :] = sums.astype(jnp.bfloat16)

        loop((CUT if row == 0 else FULL - CUT) // OWN_ROWS, body)

    def lags(r):
        lag_sums(r)
        for n in range(4):
            pack_round(r, n)
            y_copy(r, n).start()

    def relay(r):
        for n in (0, 1):
            y_copy(r, n).wait_recv()
            pack_round(r, 4 + n)
            y_copy(r, 4 + n).start()

    def total_round(r):
        def body(l):
            at = pl.multiple_of(l * OWN_ROWS, 16)
            mine = lagged[r, pl.ds(pl.multiple_of(l * HALF + y * OWN_ROWS, 16), OWN_ROWS), :]
            got = [inbox[r, d, pl.ds(at, OWN_ROWS), :].astype(jnp.float32) for d in (0, 2)]
            out[r, pl.ds(at, OWN_ROWS), :] = mine + (got[0] + got[1])

        loop(LAGS, body)

    def finish(r):
        for n in (2, 3, 4, 5):
            y_copy(r, n).wait_recv()
        total_round(r)

    def piece(slot, k, origin):
        first, pairs = WHITEN[k]
        return white.at[slot, pl.ds(FLAG_ROWS + first_pair(first, pairs, origin) * PAIR, pairs * PAIR)]

    def to_sibling(k):
        return remote(piece(0, k, zhi), piece(1, k, zhi), x_send.at[0, k], x_recv.at[0, k], ahead(1))

    def to_next(k):
        return remote(piece(0, k, zhi), piece(2, k, zhi), x_send.at[1, k], x_recv.at[1, k], ahead(2))

    def pass_up(k):
        return remote(piece(2, k, before), piece(3, k, before), x_send.at[2, k], x_recv.at[2, k], ahead(1))

    def pass_down(k):
        return remote(piece(2, k, before), piece(1, k, before), x_send.at[2, k], x_recv.at[0, k], ahead(-1))

    def pass_on(k):
        return remote(piece(2, k, before), piece(3, k, before), x_send.at[0, k], x_recv.at[2, k], ahead(1))

    def send_own(k):
        pl.when(core == 0)(to_sibling(k).start)
        pl.when(x_index != 3)(to_next(k).start)

    def forward(k):
        to_next(k).wait_recv()
        pl.when(core == 0)(pass_up(k).start)
        pl.when(core == 1)(pass_down(k).start)
        pl.when((core == 1) & (x_index != 3))(pass_on(k).start)

    def forward_early(k):
        @pl.when(x_index != 0)
        def _():
            forward(k)

    def whiten_piece(k):
        first, pairs = WHITEN[k]
        whiten(first_pair(first, pairs, zhi), pairs)
        send_own(k)

    def cross_piece(k):
        first, pairs = WHITEN[k]
        cross(0, first_pair(first, pairs, zhi), pairs)

    def receive_across(k):
        z_copy(k).wait_recv()
        if k + 2 < len(ACROSS):
            z_copy(k + 2).start()
        if k == 0:
            send_halo(0)
        first, pairs = ACROSS[k]
        magnitudes(HALO + first_pair(first, pairs, 1 - zhi) * PAIR, pairs)

    z_copy(0).start()
    z_copy(1).start()
    send_halo(1)
    for copy in flag_copies:
        copy.start()
    magnitudes(HALO + zhi * BAND_ROWS, BAND // 2)
    whiten_piece(0)
    usable_pairs(0)
    receive_across(0)
    cross_piece(0)
    halo_copy(True).wait_recv()
    halo_copy(False).wait_recv()
    magnitudes(0, SMOOTH // 2)
    magnitudes(HALO + GROUP_ROWS, SMOOTH // 2)

    @pl.when(y == 0)
    def _():
        mag[0:HALO, :] = jnp.zeros((HALO, CH), jnp.float32)

    @pl.when(y == 3)
    def _():
        mag[HALO + GROUP_ROWS :, :] = jnp.zeros((HALO, CH), jnp.float32)

    whiten_piece(1)
    cross_piece(1)
    for k in range(2, PIECES):
        receive_across(k - 1)
        whiten_piece(k)
        forward_early(k - 2)
        if k < PIECES - 1:
            cross_piece(k)
        if k == 3:
            for r in (1, 2, 3):
                flag_copies[r - 1].wait_recv()
                usable_pairs(r)

    @pl.when(x_index == 3)
    def _():
        for k in range(PIECES):
            to_next(k).start()

    forward_early(PIECES - 2)
    cross_piece(PIECES - 1)
    lags(0)
    forward_early(PIECES - 1)

    @pl.when((x_index == 3) & (core == 1))
    def _():
        for k in range(PIECES):
            pass_on(k).start()

    @pl.when(x_index == 0)
    def _():
        for k in range(PIECES):
            forward(k)

    for r in (1, 2, 3):
        if r != 2:
            for k in range(PIECES):
                remote(
                    piece(r, k, zhi), piece(r, k, zhi), x_send.at[0, k], x_recv.at[r - 1, k], ahead(1)
                ).wait_recv()
        cross(r, 0, PAIRS)
        lags(r)
        relay(r - 1)
    finish(0)
    relay(3)
    for r in (1, 2, 3):
        finish(r)

    for k in range(len(ACROSS)):
        z_copy(k).wait_send()
    halo_copy(True).wait_send()
    halo_copy(False).wait_send()
    for copy in flag_copies:
        copy.wait_send()
    for k in range(PIECES):
        to_next(k).wait_send()
        to_sibling(k).wait_send()
        pass_up(k).wait_send()
    for r in range(ROUNDS):
        for n in range(len(PARTS)):
            y_copy(r, n).wait_send()


def on_device(spectra, valid):
    groups = spectra.reshape(5, 4, BAND, 2, CH)
    raw = jnp.transpose(groups, (2, 0, 3, 1, 4)).reshape(BAND_ROWS, CH)
    flags = valid.astype(jnp.float32).reshape(5, 1, 4, CH)
    flags = jnp.broadcast_to(flags, (5, 2, 4, CH)).reshape(ROWS, CH)
    flags = jnp.pad(flags, ((0, FLAG_ROWS - ROWS), (0, 0)))
    vmem = pl.BlockSpec(memory_space=pltpu.VMEM)
    dma = pltpu.SemaphoreType.DMA
    bf16, f32 = jnp.bfloat16, jnp.float32
    out = pl.pallas_call(
        kernel,
        out_shape=jax.ShapeDtypeStruct((ROUNDS, LAGS * OWN_ROWS, CH), f32),
        in_specs=[pl.BlockSpec(memory_space=pl.ANY), vmem, vmem],
        out_specs=vmem,
        scratch_shapes=[
            pltpu.VMEM((GROUP_ROWS + 2 * HALO, CH), bf16),
            pltpu.VMEM((GROUP_ROWS + 2 * HALO, CH), f32),
            pltpu.VMEM((ROUNDS, FLAG_ROWS + GROUP_ROWS, CH), bf16),
            pltpu.VMEM((GROUP // 2, 2 * CH, CH), bf16),
            pltpu.VMEM((ROUNDS, HALF, CH), f32),
            pltpu.VMEM((HALF * STRIDE, CH), f32),
            pltpu.VMEM((ROUNDS, LAG_STORE * HALF, CH), f32),
            pltpu.VMEM((ROUNDS, 3, LAGS * OWN_ROWS, CH), bf16),
            pltpu.VMEM((ROUNDS, 3, LAGS * OWN_ROWS, CH), bf16),
            dma, dma((len(ACROSS),)), dma((len(ACROSS),)), dma((2,)), dma((2,)), dma((3,)), dma((3,)),
            dma((3, PIECES)), dma((3, PIECES)), dma((ROUNDS, 6)), dma((ROUNDS, 6)),
        ],
        compiler_params=pltpu.CompilerParams(
            collective_id=0, has_side_effects=True, vmem_limit_bytes=48 << 20
        ),
        name="correlate",
    )(raw, flags, make_table())
    return out.reshape(ROUNDS, 1, LAGS, OWN_ROWS, CH)


def solution(mesh):
    return jax.shard_map(
        on_device,
        mesh=mesh,
        in_specs=(P(None, "freq", None, "chan"), P(None, "chan")),
        out_specs=P(None, "chan", None, "freq", None),
        check_vma=False,
    )
```

```python
import math

import jax
import jax.numpy as jnp
import numpy as np
from jax import lax
from jax.experimental import pallas as pl
from jax.experimental.pallas import tpu as pltpu
from jax.sharding import PartitionSpec as P

W = 20
BINS = 272
CH = 128
LAGS = 51
ROUNDS = 4
SMOOTH = 4
BLOCKS = 64

BAND = 34
GROUP = 68
PAIRS = GROUP // 2
ROWS = 2 * W
PAIR = 2 * ROWS
HALO = SMOOTH * ROWS
BAND_ROWS = BAND * ROWS
GROUP_ROWS = GROUP * ROWS
FLAG_ROWS = 48
STRIDE = 2 * GROUP
LAG_STORE = 56
LAG_PAD = 64
OWN_ROWS = 16
HALF = 64
CUT = 26 * OWN_ROWS
FULL = LAGS * OWN_ROWS
ACROSS = ((0, 2), (12, 5), (8, 4), (4, 4), (2, 2))
WHITEN = ((2, 13), (0, 2), (15, 5), (20, 4), (24, 4), (28, 6))
PIECES = len(WHITEN)

water_level = 0.5
first_bin = 30.0
period = 600.0
MESH = pl.DeviceIdType.MESH


def make_table():
    lag_index = np.arange(LAGS, dtype=np.float32) - np.float32(LAGS // 2)
    bin_freq = np.float32(first_bin) + np.arange(BINS, dtype=np.float32)
    phase = np.float32(2.0 * math.pi) * lag_index[:, None] * bin_freq[None, :] / np.float32(period)
    both = np.stack([np.cos(phase), -np.sin(phase)], axis=1).reshape(LAGS, 2, 4, GROUP)
    table = np.zeros((4, LAG_PAD, 2, GROUP), np.float32)
    table[:, :LAGS] = both.transpose(2, 0, 1, 3)
    return jnp.asarray(table.reshape(4, LAG_PAD, STRIDE), jnp.bfloat16)


def roll4(x):
    return pltpu.roll(x, 4, axis=1)


def loop(count, body):
    lax.fori_loop(0, count, lambda n, carry: (body(n), carry)[1], 0, unroll=unrolled(count))


def unrolled(count):
    return max(n for n in range(1, 18) if count % n == 0)


def kernel(
    raw, usable, tables, out,
    band, mag, white, lhs, inverse, spread, lagged, outbox, inbox, detour, flags_in, flags, table,
    load_sem, z_send, z_recv, h_send, h_recv, f_send, f_recv, x_send, x_recv, w_send, w_recv, y_send, y_recv,
):
    i, j = lax.axis_index("chan"), lax.axis_index("freq")
    y, zhi = j // 2, j % 2
    core = i % 2
    x_index = (i // 2) % 4
    z_index = zhi * 8 + i // 8
    before = jnp.where(x_index == 0, ((z_index + 15) % 16) // 8, zhi)

    def ahead(r):
        t = i + r + BLOCKS
        flip = (t // BLOCKS + 1) % 2
        return {"chan": t % BLOCKS, "freq": j + flip * (1 - 2 * zhi)}

    def along_y(d):
        return {"chan": i, "freq": ((y + d) % 4) * 2 + zhi}

    across = {"chan": i, "freq": j + 1 - 2 * zhi}

    def first_pair(first, pairs, origin):
        return first + origin * (PAIRS - 2 * first - pairs)

    def remote(src, dst, send, recv, device):
        return pltpu.make_async_remote_copy(
            src_ref=src, dst_ref=dst, send_sem=send, recv_sem=recv,
            device_id=device, device_id_type=MESH,
        )

    loads = [
        pltpu.make_async_copy(usable, flags_in, load_sem.at[0]),
        pltpu.make_async_copy(raw, band.at[pl.ds(HALO + zhi * BAND_ROWS, BAND_ROWS)], load_sem.at[1]),
        pltpu.make_async_copy(tables.at[y], table, load_sem.at[2]),
    ]
    for load in loads:
        load.start()
    barrier = pltpu.get_barrier_semaphore()
    partners = [across] + [along_y(d) for d in (1, 3)]
    partners += [ahead(r) for r in (1, 2, 3, 4, -1, -2, -3, -4)]
    for partner in partners:
        pl.semaphore_signal(barrier, inc=1, device_id=partner, device_id_type=MESH)
    loads[0].wait()
    once = flags_in[...].astype(jnp.float32)
    for g in range(5):
        flags[8 * g : 8 * g + 4, :] = once[4 * g : 4 * g + 4, :]
        flags[8 * g + 4 : 8 * g + 8, :] = once[4 * g : 4 * g + 4, :]
    flags[ROWS:FLAG_ROWS, :] = jnp.zeros((FLAG_ROWS - ROWS, CH), jnp.float32)
    white[0, 0:FLAG_ROWS, :] = flags[...].astype(jnp.bfloat16)
    for load in loads[1:]:
        load.wait()
    pl.semaphore_wait(barrier, len(partners))

    def z_copy(k):
        first, pairs = ACROSS[k]
        here = band.at[pl.ds(HALO + first_pair(first, pairs, zhi) * PAIR, pairs * PAIR)]
        return remote(here, here, z_send.at[k], z_recv.at[k], across)

    def halo_copy(top):
        src = GROUP_ROWS if top else HALO
        dst = 0 if top else HALO + GROUP_ROWS
        k = 0 if top else 1
        return remote(
            band.at[pl.ds(src, HALO)], band.at[pl.ds(dst, HALO)],
            h_send.at[k], h_recv.at[k], along_y(1 if top else 3),
        )

    def send_halo(own):
        pl.when(zhi == own)(halo_copy(True).start)
        pl.when(zhi != own)(halo_copy(False).start)

    flag_copies = [
        remote(
            white.at[0, pl.ds(0, FLAG_ROWS)], white.at[r, pl.ds(0, FLAG_ROWS)],
            f_send.at[r - 1], f_recv.at[r - 1], ahead(r),
        )
        for r in (1, 2, 3)
    ]

    sublane = lax.broadcasted_iota(jnp.int32, (1, 8, CH), 1)
    lane = lax.broadcasted_iota(jnp.int32, (1, 8, CH), 2)
    sign = jnp.where(sublane < 4, -1.0, 1.0)
    first_half = (lane % 32) < 16
    valid = flags[0:ROWS, :]

    def magnitudes(row, pairs):
        def body(p):
            at = pl.multiple_of(row + p * PAIR, 16)
            v = band[pl.ds(at, PAIR), :].astype(jnp.float32).reshape(10, 8, CH)
            square = v * v
            m = jnp.sqrt(square + roll4(square))
            mag[pl.ds(at, PAIR), :] = m.reshape(PAIR, CH)

        loop(pairs, body)

    def whiten(start, pairs):
        def body(p):
            pair = start + p
            row = pl.multiple_of(pair * PAIR, 16)
            m = [mag[pl.ds(pl.multiple_of(row + t * ROWS, 8), ROWS), :] for t in range(10)]
            inner = ((m[1] + m[2]) + (m[3] + m[4])) + ((m[5] + m[6]) + (m[7] + m[8]))
            outs = []
            for t in range(2):
                bin_index = y * GROUP + 2 * pair + t
                count = (
                    jnp.minimum(bin_index + SMOOTH, BINS - 1) - jnp.maximum(bin_index - SMOOTH, 0) + 1
                ).astype(jnp.float32)
                total = inner + (m[0] if t == 0 else m[9])
                water = jnp.maximum(total / jnp.full((1, CH), count, jnp.float32), water_level)
                outs.append(valid / water)
            factor = jnp.concatenate(outs, axis=0)
            v = band[pl.ds(pl.multiple_of(row + HALO, 16), PAIR), :].astype(jnp.float32)
            w = (v * factor).astype(jnp.bfloat16)
            white[0, pl.ds(pl.multiple_of(FLAG_ROWS + row, 16), PAIR), :] = w
            a1 = pltpu.roll(w.astype(jnp.float32).reshape(10, 8, CH), 112 * zhi, axis=2)
            a2 = pltpu.roll(roll4(a1) * sign, 16, axis=2)
            both = jnp.where(first_half, a1, a2).reshape(PAIR, CH)
            turned = jnp.transpose(both)
            column = lax.broadcasted_iota(jnp.int32, (CH, PAIR), 1)
            lhs[pair, 0:CH, 0:PAIR] = jnp.where(column < ROWS, turned, 0.0).astype(jnp.bfloat16)
            lhs[pair, CH : 2 * CH, 0:PAIR] = jnp.where(column < ROWS, 0.0, turned).astype(jnp.bfloat16)

        loop(pairs, body)

    def cross(r, start, pairs):
        def body(p):
            pair = start + p
            rhs = white[r, pl.ds(pl.multiple_of(FLAG_ROWS + pair * PAIR, 16), PAIR), :]
            c = jnp.dot(lhs[pair, :, 0:PAIR], rhs, preferred_element_type=jnp.float32)
            for g in range(4):
                scale = inverse[r, g * 16 : (g + 1) * 16, :]
                for t in range(2):
                    for part in range(2):
                        at = t * CH + g * 32 + part * 16
                        row = g * 16 * STRIDE + part * GROUP + 2 * pair + t
                        spread[pl.ds(row, 16, stride=STRIDE), :] = c[at : at + 16, :] * scale

        loop(pairs, body)

    def usable_pairs(r):
        mine = white[0, 0:FLAG_ROWS, :].astype(jnp.float32)
        mine = pltpu.roll(mine, 112 * zhi, axis=1)
        n = jnp.dot(
            jnp.transpose(mine).astype(jnp.bfloat16), white[r, 0:FLAG_ROWS, :],
            preferred_element_type=jnp.float32,
        )
        scale = 1.0 / jnp.maximum(n * 0.5, 1.0)
        for g in range(4):
            inverse[r, g * 16 : (g + 1) * 16, :] = scale[g * 32 : g * 32 + 16, :]

    def lag_sums(r, to):
        tab = table[...]

        def body(p):
            a = OWN_ROWS * to + 2 * p
            s0 = spread[pl.ds(pl.multiple_of(a * STRIDE, 8), STRIDE), :].astype(jnp.bfloat16)
            s1 = spread[pl.ds(pl.multiple_of((a + 1) * STRIDE, 8), STRIDE), :].astype(jnp.bfloat16)
            both = jnp.concatenate([s0, s1], axis=1)
            c = jnp.dot(tab, both, preferred_element_type=jnp.float32)
            lagged[r, pl.ds(a, LAG_STORE, stride=HALF), :] = c[0:LAG_STORE, 0:CH]
            lagged[r, pl.ds(a + 1, LAG_STORE, stride=HALF), :] = c[0:LAG_STORE, CH : 2 * CH]

        loop(OWN_ROWS // 2, body)

    PARTS = ((2, 0, 1), (2, CUT, 3), (1, CUT, 1), (3, 0, 3), (1, 0, 1), (3, CUT, 3))

    def y_copy(r, n):
        d, row, way = PARTS[n]
        part = pl.ds(row, CUT if row == 0 else FULL - CUT)
        return remote(
            outbox.at[r, d - 1, part], inbox.at[r, d - 1, part], y_send.at[r, n], y_recv.at[r, n], along_y(way)
        )

    def pack_round(r, n):
        d, row, _ = PARTS[n]
        to = (y + d) % 4

        def body(l):
            at = pl.multiple_of(row + l * OWN_ROWS, 16)
            from_row = pl.multiple_of(row // OWN_ROWS * HALF + l * HALF + to * OWN_ROWS, 16)
            sums = lagged[r, pl.ds(from_row, OWN_ROWS), :]
            if n >= 4:
                sums = sums + inbox[r, 1, pl.ds(at, OWN_ROWS), :].astype(jnp.float32)
            outbox[r, d - 1, pl.ds(at, OWN_ROWS), :] = sums.astype(jnp.bfloat16)

        loop((CUT if row == 0 else FULL - CUT) // OWN_ROWS, body)

    def lags(r):
        lag_sums(r, (y + 2) % 4)
        for n in (0, 1):
            pack_round(r, n)
            y_copy(r, n).start()
        for n in (2, 3):
            lag_sums(r, (y + PARTS[n][0]) % 4)
            pack_round(r, n)
            y_copy(r, n).start()
        lag_sums(r, y)

    def relay(r):
        for n in (0, 1):
            y_copy(r, n).wait_recv()
            pack_round(r, 4 + n)
            y_copy(r, 4 + n).start()

    def total_round(r):
        def body(l):
            at = pl.multiple_of(l * OWN_ROWS, 16)
            mine = lagged[r, pl.ds(pl.multiple_of(l * HALF + y * OWN_ROWS, 16), OWN_ROWS), :]
            got = [inbox[r, d, pl.ds(at, OWN_ROWS), :].astype(jnp.float32) for d in (0, 2)]
            out[r, pl.ds(at, OWN_ROWS), :] = mine + (got[0] + got[1])

        loop(LAGS, body)

    def finish(r):
        for n in (2, 3, 4, 5):
            y_copy(r, n).wait_recv()
        total_round(r)

    def piece(slot, k, origin):
        first, pairs = WHITEN[k]
        return white.at[slot, pl.ds(FLAG_ROWS + first_pair(first, pairs, origin) * PAIR, pairs * PAIR)]

    def to_sibling(k):
        return remote(piece(0, k, zhi), piece(1, k, zhi), x_send.at[0, k], x_recv.at[0, k], ahead(1))

    def to_next(k):
        return remote(piece(0, k, zhi), piece(2, k, zhi), x_send.at[1, k], x_recv.at[1, k], ahead(2))

    def pass_up(k):
        return remote(piece(2, k, before), piece(3, k, before), x_send.at[2, k], x_recv.at[2, k], ahead(1))

    def pass_down(k):
        return remote(piece(2, k, before), piece(1, k, before), x_send.at[2, k], x_recv.at[0, k], ahead(-1))

    def pass_on(k):
        return remote(piece(2, k, before), piece(3, k, before), x_send.at[0, k], x_recv.at[2, k], ahead(1))

    def detour_rows(k):
        first, pairs = WHITEN[k]
        return detour.at[pl.ds(first_pair(first, pairs, zhi) * PAIR, pairs * PAIR)]

    def detour_in(k):
        return remote(piece(0, k, zhi), detour_rows(k), w_send.at[k], w_recv.at[k], ahead(-2))

    def detour_out(k):
        return remote(detour_rows(k), piece(2, k, zhi), w_send.at[k], x_recv.at[1, k], ahead(4))

    last_odd = (x_index == 3) & (core == 1)
    last_even = (x_index == 3) & (core == 0)
    helper = (x_index == 2) & (core == 1)

    def send_own(k):
        pl.when(core == 0)(to_sibling(k).start)
        pl.when(x_index != 3)(to_next(k).start)
        pl.when(last_odd)(detour_in(k).start)

    def help_out(k):
        detour_in(k).wait_recv()
        detour_out(k).start()

    def forward(k):
        to_next(k).wait_recv()
        pl.when(core == 0)(pass_up(k).start)
        pl.when(core == 1)(pass_down(k).start)
        pl.when((core == 1) & (x_index != 3))(pass_on(k).start)

    def forward_early(k):
        @pl.when(x_index != 0)
        def _():
            forward(k)

    def whiten_piece(k):
        first, pairs = WHITEN[k]
        whiten(first_pair(first, pairs, zhi), pairs)
        send_own(k)

    def cross_piece(k):
        first, pairs = WHITEN[k]
        cross(0, first_pair(first, pairs, zhi), pairs)

    def receive_across(k):
        z_copy(k).wait_recv()
        if k == 0:
            send_halo(0)
        first, pairs = ACROSS[k]
        magnitudes(HALO + first_pair(first, pairs, 1 - zhi) * PAIR, pairs)

    for k in range(len(ACROSS)):
        z_copy(k).start()
    send_halo(1)
    for copy in flag_copies:
        copy.start()
    magnitudes(HALO + zhi * BAND_ROWS, BAND // 2)
    whiten_piece(0)
    usable_pairs(0)
    receive_across(0)
    cross_piece(0)
    halo_copy(True).wait_recv()
    halo_copy(False).wait_recv()
    magnitudes(0, SMOOTH // 2)
    magnitudes(HALO + GROUP_ROWS, SMOOTH // 2)

    @pl.when(y == 0)
    def _():
        mag[0:HALO, :] = jnp.zeros((HALO, CH), jnp.float32)

    @pl.when(y == 3)
    def _():
        mag[HALO + GROUP_ROWS :, :] = jnp.zeros((HALO, CH), jnp.float32)

    whiten_piece(1)
    cross_piece(1)
    for k in range(2, PIECES):
        receive_across(k - 1)
        whiten_piece(k)
        forward_early(k - 2)
        if k < PIECES - 1:
            cross_piece(k)
        if k == 3:
            for r in (1, 2, 3):
                flag_copies[r - 1].wait_recv()
                usable_pairs(r)

    @pl.when(last_even)
    def _():
        for k in range(PIECES):
            to_next(k).start()

    @pl.when(helper)
    def _():
        for k in range(PIECES - 1):
            help_out(k)

    forward_early(PIECES - 2)
    cross_piece(PIECES - 1)
    lags(0)
    pl.when(helper)(lambda: help_out(PIECES - 1))
    forward_early(PIECES - 1)

    @pl.when(last_odd)
    def _():
        for k in range(PIECES):
            pass_on(k).start()

    def forward_late():
        for k in range(PIECES):
            forward(k)

    def receive(slot):
        for k in range(PIECES):
            remote(
                piece(slot, k, zhi), piece(slot, k, zhi), x_send.at[0, k], x_recv.at[slot - 1, k], ahead(1)
            ).wait_recv()

    second, third = 2 - core, 1 + core
    pl.when((x_index == 0) & (core == 0))(forward_late)
    pl.when(core == 1)(lambda: receive(1))
    cross(second, 0, PAIRS)
    lags(second)
    relay(0)
    pl.when((x_index == 0) & (core == 1))(forward_late)
    pl.when(core == 0)(lambda: receive(1))
    cross(third, 0, PAIRS)
    lags(third)
    relay(second)
    receive(3)
    cross(3, 0, PAIRS)
    lags(3)
    relay(third)
    finish(0)
    finish(second)
    relay(3)
    finish(third)
    finish(3)

    for k in range(len(ACROSS)):
        z_copy(k).wait_send()
    halo_copy(True).wait_send()
    halo_copy(False).wait_send()
    for copy in flag_copies:
        copy.wait_send()
    for k in range(PIECES):
        pl.when(jnp.logical_not(last_odd))(to_next(k).wait_send)
        pl.when(last_odd | helper)(detour_in(k).wait_send)
        to_sibling(k).wait_send()
        pass_up(k).wait_send()
    for r in range(ROUNDS):
        for n in range(len(PARTS)):
            y_copy(r, n).wait_send()


def on_device(spectra, valid):
    groups = spectra.reshape(5, 4, BAND, 2, CH)
    raw = jnp.transpose(groups, (2, 0, 3, 1, 4)).reshape(BAND_ROWS, CH)
    vmem = pl.BlockSpec(memory_space=pltpu.VMEM)
    dma = pltpu.SemaphoreType.DMA
    bf16, f32 = jnp.bfloat16, jnp.float32
    out = pl.pallas_call(
        kernel,
        out_shape=jax.ShapeDtypeStruct((ROUNDS, LAGS * OWN_ROWS, CH), f32),
        in_specs=[pl.BlockSpec(memory_space=pl.ANY)] * 3,
        out_specs=vmem,
        scratch_shapes=[
            pltpu.VMEM((GROUP_ROWS + 2 * HALO, CH), bf16),
            pltpu.VMEM((GROUP_ROWS + 2 * HALO, CH), f32),
            pltpu.VMEM((ROUNDS, FLAG_ROWS + GROUP_ROWS, CH), bf16),
            pltpu.VMEM((GROUP // 2, 2 * CH, CH), bf16),
            pltpu.VMEM((ROUNDS, HALF, CH), f32),
            pltpu.VMEM((HALF * STRIDE, CH), f32),
            pltpu.VMEM((ROUNDS, LAG_STORE * HALF, CH), f32),
            pltpu.VMEM((ROUNDS, 3, LAGS * OWN_ROWS, CH), bf16),
            pltpu.VMEM((ROUNDS, 3, LAGS * OWN_ROWS, CH), bf16),
            pltpu.VMEM((GROUP_ROWS, CH), bf16),
            pltpu.VMEM((W, CH), jnp.int32),
            pltpu.VMEM((FLAG_ROWS, CH), f32),
            pltpu.VMEM((LAG_PAD, STRIDE), bf16),
            dma((3,)), dma((len(ACROSS),)), dma((len(ACROSS),)), dma((2,)), dma((2,)), dma((3,)), dma((3,)),
            dma((3, PIECES)), dma((3, PIECES)), dma((PIECES,)), dma((PIECES,)), dma((ROUNDS, 6)), dma((ROUNDS, 6)),
        ],
        compiler_params=pltpu.CompilerParams(
            collective_id=0, has_side_effects=True, vmem_limit_bytes=48 << 20
        ),
        name="correlate",
    )(raw, valid, make_table())
    return out.reshape(ROUNDS, 1, LAGS, OWN_ROWS, CH)


def solution(mesh):
    return jax.shard_map(
        on_device,
        mesh=mesh,
        in_specs=(P(None, "freq", None, "chan"), P(None, "chan")),
        out_specs=P(None, "chan", None, "freq", None),
        check_vma=False,
    )
```

```python
import math

import jax
import jax.numpy as jnp
from jax import lax
from jax.experimental import pallas as pl
from jax.experimental.pallas import tpu as pltpu
from jax.sharding import PartitionSpec as P

W = 20
BINS = 272
CH = 128
LAGS = 51
ROUNDS = 4
SMOOTH = 4
BLOCKS = 64

BAND = 34
GROUP = 68
PAIRS = GROUP // 2
ROWS = 2 * W
PAIR = 2 * ROWS
HALO = SMOOTH * ROWS
BAND_ROWS = BAND * ROWS
GROUP_ROWS = GROUP * ROWS
FLAG_ROWS = 48
STRIDE = 2 * GROUP
LAG_STORE = 56
LAG_PAD = 64
OWN_ROWS = 16
HALF = 64
CUT = 26 * OWN_ROWS
FULL = LAGS * OWN_ROWS
ACROSS = ((0, 2), (12, 5), (8, 4), (4, 4), (2, 2))
WHITEN = ((2, 13), (0, 2), (15, 5), (20, 4), (24, 4), (28, 6))
PIECES = len(WHITEN)
EVEN_BY = (0, 1, 1, 1, 2, 2)
TURN = 1

water_level = 0.5
first_bin = 30.0
period = 600.0
MESH = pl.DeviceIdType.MESH


def roll4(x):
    return pltpu.roll(x, 4, axis=1)


def loop(count, body):
    lax.fori_loop(0, count, lambda n, carry: (body(n), carry)[1], 0, unroll=unrolled(count))


def unrolled(count):
    return max(n for n in range(1, 18) if count % n == 0)


def kernel(
    raw, usable, out,
    band, mag, white, lhs, inverse, spread, lagged, outbox, inbox, detour, flags_in, flags, table,
    load_sem, go_sem, z_send, z_recv, h_send, h_recv, f_send, f_recv, x_send, x_recv, w_send, w_recv, y_send, y_recv,
):
    i, j = lax.axis_index("chan"), lax.axis_index("freq")
    y, zhi = j // 2, j % 2
    core = i % 2
    x_index = (i // 2) % 4
    z_index = zhi * 8 + i // 8
    before = jnp.where(x_index == 0, ((z_index + 15) % 16) // 8, zhi)

    def ahead(r):
        t = i + r + BLOCKS
        flip = (t // BLOCKS + 1) % 2
        return {"chan": t % BLOCKS, "freq": j + flip * (1 - 2 * zhi)}

    def along_y(d):
        return {"chan": i, "freq": ((y + d) % 4) * 2 + zhi}

    across = {"chan": i, "freq": j + 1 - 2 * zhi}
    sibling = {"chan": i + 1 - 2 * core, "freq": j}

    def first_pair(first, pairs, origin):
        return first + origin * (PAIRS - 2 * first - pairs)

    def remote(src, dst, send, recv, device):
        return pltpu.make_async_remote_copy(
            src_ref=src, dst_ref=dst, send_sem=send, recv_sem=recv,
            device_id=device, device_id_type=MESH,
        )

    loads = [
        pltpu.make_async_copy(usable, flags_in, load_sem.at[0]),
        pltpu.make_async_copy(raw, band.at[pl.ds(HALO + zhi * BAND_ROWS, BAND_ROWS)], load_sem.at[1]),
    ]
    for load in loads:
        load.start()
    barrier = pltpu.get_barrier_semaphore()
    partners = [across] + [along_y(d) for d in (1, 3)]
    partners += [ahead(r) for r in (1, 2, 3, 4, 6, -1, -2, -3, -4, -6)]
    for partner in partners:
        pl.semaphore_signal(barrier, inc=1, device_id=partner, device_id_type=MESH)
    loads[0].wait()
    once = flags_in[...].astype(jnp.float32)
    for g in range(5):
        flags[8 * g : 8 * g + 4, :] = once[4 * g : 4 * g + 4, :]
        flags[8 * g + 4 : 8 * g + 8, :] = once[4 * g : 4 * g + 4, :]
    flags[ROWS:FLAG_ROWS, :] = jnp.zeros((FLAG_ROWS - ROWS, CH), jnp.float32)
    white[0, 0:FLAG_ROWS, :] = flags[...].astype(jnp.bfloat16)
    for load in loads[1:]:
        load.wait()
    pl.semaphore_wait(barrier, len(partners))

    def z_copy(k):
        first, pairs = ACROSS[k]
        here = band.at[pl.ds(HALO + first_pair(first, pairs, zhi) * PAIR, pairs * PAIR)]
        return remote(here, here, z_send.at[k], z_recv.at[k], across)

    def halo_copy(top):
        src = GROUP_ROWS if top else HALO
        dst = 0 if top else HALO + GROUP_ROWS
        k = 0 if top else 1
        return remote(
            band.at[pl.ds(src, HALO)], band.at[pl.ds(dst, HALO)],
            h_send.at[k], h_recv.at[k], along_y(1 if top else 3),
        )

    def send_halo(own):
        pl.when(zhi == own)(halo_copy(True).start)
        pl.when(zhi != own)(halo_copy(False).start)

    flag_copies = [
        remote(
            white.at[0, pl.ds(0, FLAG_ROWS)], white.at[r, pl.ds(0, FLAG_ROWS)],
            f_send.at[r - 1], f_recv.at[r - 1], ahead(r),
        )
        for r in (1, 2, 3)
    ]

    sublane = lax.broadcasted_iota(jnp.int32, (1, 8, CH), 1)
    lane = lax.broadcasted_iota(jnp.int32, (1, 8, CH), 2)
    sign = jnp.where(sublane < 4, -1.0, 1.0)
    first_half = (lane % 32) < 16
    valid = flags[0:ROWS, :]

    def make_table():
        lag = lax.broadcasted_iota(jnp.int32, (LAG_PAD, STRIDE), 0)
        column = lax.broadcasted_iota(jnp.int32, (LAG_PAD, STRIDE), 1)
        bins = y * GROUP + jnp.where(column < GROUP, column, column - GROUP)
        lag_index = lag.astype(jnp.float32) - float(LAGS // 2)
        bin_freq = first_bin + bins.astype(jnp.float32)
        phase_angle = 2.0 * math.pi * lag_index * bin_freq / period
        both = jnp.where(column < GROUP, jnp.cos(phase_angle), -jnp.sin(phase_angle))
        table[...] = jnp.where(lag < LAGS, both, 0.0).astype(jnp.bfloat16)

    def magnitudes(row, pairs):
        def body(p):
            at = pl.multiple_of(row + p * PAIR, 16)
            v = band[pl.ds(at, PAIR), :].astype(jnp.float32).reshape(10, 8, CH)
            square = v * v
            m = jnp.sqrt(square + roll4(square))
            mag[pl.ds(at, PAIR), :] = m.reshape(PAIR, CH)

        loop(pairs, body)

    def whiten(start, pairs):
        def body(p):
            pair = start + p
            row = pl.multiple_of(pair * PAIR, 16)
            m = [mag[pl.ds(pl.multiple_of(row + t * ROWS, 8), ROWS), :] for t in range(10)]
            inner = ((m[1] + m[2]) + (m[3] + m[4])) + ((m[5] + m[6]) + (m[7] + m[8]))
            outs = []
            for t in range(2):
                bin_index = y * GROUP + 2 * pair + t
                count = (
                    jnp.minimum(bin_index + SMOOTH, BINS - 1) - jnp.maximum(bin_index - SMOOTH, 0) + 1
                ).astype(jnp.float32)
                total = inner + (m[0] if t == 0 else m[9])
                water = jnp.maximum(total / jnp.full((1, CH), count, jnp.float32), water_level)
                outs.append(valid / water)
            factor = jnp.concatenate(outs, axis=0)
            v = band[pl.ds(pl.multiple_of(row + HALO, 16), PAIR), :].astype(jnp.float32)
            w = (v * factor).astype(jnp.bfloat16)
            white[0, pl.ds(pl.multiple_of(FLAG_ROWS + row, 16), PAIR), :] = w
            a1 = pltpu.roll(w.astype(jnp.float32).reshape(10, 8, CH), 112 * zhi, axis=2)
            a2 = pltpu.roll(roll4(a1) * sign, 16, axis=2)
            both = jnp.where(first_half, a1, a2).reshape(PAIR, CH)
            turned = jnp.transpose(both)
            column = lax.broadcasted_iota(jnp.int32, (CH, PAIR), 1)
            lhs[pair, 0:CH, 0:PAIR] = jnp.where(column < ROWS, turned, 0.0).astype(jnp.bfloat16)
            lhs[pair, CH : 2 * CH, 0:PAIR] = jnp.where(column < ROWS, 0.0, turned).astype(jnp.bfloat16)

        loop(pairs, body)

    def cross(r, start, pairs):
        def body(p):
            pair = start + p
            rhs = white[r, pl.ds(pl.multiple_of(FLAG_ROWS + pair * PAIR, 16), PAIR), :]
            c = jnp.dot(lhs[pair, :, 0:PAIR], rhs, preferred_element_type=jnp.float32)
            for g in range(4):
                scale = inverse[r, g * 16 : (g + 1) * 16, :]
                for t in range(2):
                    for part in range(2):
                        at = t * CH + g * 32 + part * 16
                        row = g * 16 * STRIDE + part * GROUP + 2 * pair + t
                        spread[pl.ds(row, 16, stride=STRIDE), :] = c[at : at + 16, :] * scale

        loop(pairs, body)

    def usable_pairs(r):
        mine = white[0, 0:FLAG_ROWS, :].astype(jnp.float32)
        mine = pltpu.roll(mine, 112 * zhi, axis=1)
        n = jnp.dot(
            jnp.transpose(mine).astype(jnp.bfloat16), white[r, 0:FLAG_ROWS, :],
            preferred_element_type=jnp.float32,
        )
        scale = 1.0 / jnp.maximum(n * 0.5, 1.0)
        for g in range(4):
            inverse[r, g * 16 : (g + 1) * 16, :] = scale[g * 32 : g * 32 + 16, :]

    def lag_sums(r, to):
        tab = table[...]

        def body(p):
            a = OWN_ROWS * to + 2 * p
            s0 = spread[pl.ds(pl.multiple_of(a * STRIDE, 8), STRIDE), :].astype(jnp.bfloat16)
            s1 = spread[pl.ds(pl.multiple_of((a + 1) * STRIDE, 8), STRIDE), :].astype(jnp.bfloat16)
            both = jnp.concatenate([s0, s1], axis=1)
            c = jnp.dot(tab, both, preferred_element_type=jnp.float32)
            lagged[r, pl.ds(a, LAG_STORE, stride=HALF), :] = c[0:LAG_STORE, 0:CH]
            lagged[r, pl.ds(a + 1, LAG_STORE, stride=HALF), :] = c[0:LAG_STORE, CH : 2 * CH]

        loop(OWN_ROWS // 2, body)

    PARTS = ((2, 0, 1), (2, CUT, 3), (1, CUT, 1), (3, 0, 3), (1, 0, 1), (3, CUT, 3))

    def y_copy(r, n):
        d, row, way = PARTS[n]
        part = pl.ds(row, CUT if row == 0 else FULL - CUT)
        return remote(
            outbox.at[r, d - 1, part], inbox.at[r, d - 1, part], y_send.at[r, n], y_recv.at[r, n], along_y(way)
        )

    def pack_round(r, n):
        d, row, _ = PARTS[n]
        to = (y + d) % 4

        def body(l):
            at = pl.multiple_of(row + l * OWN_ROWS, 16)
            from_row = pl.multiple_of(row // OWN_ROWS * HALF + l * HALF + to * OWN_ROWS, 16)
            sums = lagged[r, pl.ds(from_row, OWN_ROWS), :]
            if n >= 4:
                sums = sums + inbox[r, 1, pl.ds(at, OWN_ROWS), :].astype(jnp.float32)
            outbox[r, d - 1, pl.ds(at, OWN_ROWS), :] = sums.astype(jnp.bfloat16)

        loop((CUT if row == 0 else FULL - CUT) // OWN_ROWS, body)

    def lags(r):
        lag_sums(r, (y + 2) % 4)
        for n in (0, 1):
            pack_round(r, n)
            y_copy(r, n).start()
        for n in (2, 3):
            lag_sums(r, (y + PARTS[n][0]) % 4)
            pack_round(r, n)
            y_copy(r, n).start()
        lag_sums(r, y)

    def relay(r):
        for n in (0, 1):
            y_copy(r, n).wait_recv()
            pack_round(r, 4 + n)
            y_copy(r, 4 + n).start()

    def total_round(r):
        def body(l):
            at = pl.multiple_of(l * OWN_ROWS, 16)
            mine = lagged[r, pl.ds(pl.multiple_of(l * HALF + y * OWN_ROWS, 16), OWN_ROWS), :]
            got = [inbox[r, d, pl.ds(at, OWN_ROWS), :].astype(jnp.float32) for d in (0, 2)]
            out[r, pl.ds(at, OWN_ROWS), :] = mine + (got[0] + got[1])

        loop(LAGS, body)

    def finish(r):
        for n in (2, 3, 4, 5):
            y_copy(r, n).wait_recv()
        total_round(r)

    def piece(slot, k, origin):
        first, pairs = WHITEN[k]
        return white.at[slot, pl.ds(FLAG_ROWS + first_pair(first, pairs, origin) * PAIR, pairs * PAIR)]

    def to_sibling(k):
        return remote(piece(0, k, zhi), piece(1, k, zhi), x_send.at[0, k], x_recv.at[0, k], ahead(1))

    def to_next(k):
        return remote(piece(0, k, zhi), piece(2, k, zhi), x_send.at[1, k], x_recv.at[1, k], ahead(2))

    def pass_up(k):
        return remote(piece(2, k, before), piece(3, k, before), x_send.at[2, k], x_recv.at[2, k], ahead(1))

    def pass_down(k):
        return remote(piece(2, k, before), piece(1, k, before), x_send.at[2, k], x_recv.at[0, k], ahead(-1))

    def pass_on(k):
        return remote(piece(2, k, before), piece(3, k, before), x_send.at[0, k], x_recv.at[2, k], ahead(1))

    def detour_rows(k):
        first, pairs = WHITEN[k]
        return detour.at[pl.ds(first_pair(first, pairs, zhi) * PAIR, pairs * PAIR)]

    def detour_in(k):
        return remote(piece(0, k, zhi), detour_rows(k), w_send.at[k], w_recv.at[k], ahead(-4))

    def detour_out(k):
        return remote(detour_rows(k), piece(2, k, zhi), w_send.at[k], x_recv.at[1, k], ahead(6))

    def jump(k):
        return remote(piece(0, k, zhi), piece(3, k, zhi), w_send.at[k], x_recv.at[2, k], ahead(3))

    def detour_even(k):
        chips = EVEN_BY[k]
        return remote(piece(0, k, zhi), detour_rows(k), w_send.at[k], w_recv.at[k], ahead(-2 * chips))

    def detour_even_out(k):
        chips = EVEN_BY[k]
        return remote(detour_rows(k), piece(2, k, zhi), w_send.at[k], x_recv.at[1, k], ahead(2 + 2 * chips))

    def even_helper(k):
        return (x_index == 3 - EVEN_BY[k]) & (core == 0)

    def help_even(k):
        if EVEN_BY[k]:
            @pl.when(even_helper(k))
            def _():
                detour_even(k).wait_recv()
                detour_even_out(k).start()

    last_odd = (x_index == 3) & (core == 1)
    last_even = (x_index == 3) & (core == 0)
    jumper = (x_index == 2) & (core == 1)
    helper = (x_index == 1) & (core == 1)

    def send_own(k):
        pl.when(core == 0)(to_sibling(k).start)
        pl.when(x_index != 3)(to_next(k).start)
        pl.when(last_even)(detour_even(k).start if EVEN_BY[k] else to_next(k).start)
        pl.when(last_odd)(detour_in(k).start)

    def help_out(k):
        detour_in(k).wait_recv()
        detour_out(k).start()

    def go_on():
        pl.semaphore_signal(go_sem, inc=1, device_id=sibling, device_id_type=MESH)

    def forward(k):
        to_next(k).wait_recv()
        pl.when(core == 0)(pass_up(k).start)
        pl.when(core == 1)(pass_down(k).start)
        pl.when((core == 1) & (x_index != 3))(pass_on(k).start)

    def forward_early(k):
        @pl.when(x_index != 0)
        def _():
            forward(k)

    def whiten_piece(k):
        first, pairs = WHITEN[k]
        whiten(first_pair(first, pairs, zhi), pairs)
        send_own(k)

    def cross_piece(k):
        first, pairs = WHITEN[k]
        cross(0, first_pair(first, pairs, zhi), pairs)

    def receive_across(k):
        z_copy(k).wait_recv()
        if k == 0:
            send_halo(0)
        first, pairs = ACROSS[k]
        magnitudes(HALO + first_pair(first, pairs, 1 - zhi) * PAIR, pairs)

    z_copy(0).start()

    @pl.when(core == 0)
    def _():
        for k in range(1, len(ACROSS)):
            z_copy(k).start()

    send_halo(1)
    for copy in flag_copies:
        copy.start()
    magnitudes(HALO + zhi * BAND_ROWS, BAND // 2)
    whiten_piece(0)
    make_table()
    usable_pairs(0)
    receive_across(0)
    cross_piece(0)
    halo_copy(True).wait_recv()
    halo_copy(False).wait_recv()
    magnitudes(0, SMOOTH // 2)
    magnitudes(HALO + GROUP_ROWS, SMOOTH // 2)

    @pl.when(y == 0)
    def _():
        mag[0:HALO, :] = jnp.zeros((HALO, CH), jnp.float32)

    @pl.when(y == 3)
    def _():
        mag[HALO + GROUP_ROWS :, :] = jnp.zeros((HALO, CH), jnp.float32)

    whiten_piece(1)
    cross_piece(1)

    @pl.when(core == 1)
    def _():
        pl.semaphore_wait(go_sem, 1)
        for k in range(1, len(ACROSS)):
            z_copy(k).start()

    for k in range(2, PIECES):
        receive_across(k - 1)
        if k - 1 == TURN:
            pl.when(core == 0)(go_on)
        whiten_piece(k)
        forward_early(k - 2)
        help_even(k - 2)
        if k < PIECES - 1:
            cross_piece(k)
        if k == 3:
            for r in (1, 2, 3):
                flag_copies[r - 1].wait_recv()
                usable_pairs(r)

    @pl.when(jumper)
    def _():
        for k in range(PIECES):
            jump(k).start()

    @pl.when(helper)
    def _():
        for k in range(PIECES - 1):
            help_out(k)

    forward_early(PIECES - 2)
    help_even(PIECES - 2)
    cross_piece(PIECES - 1)
    lags(0)
    pl.when(helper)(lambda: help_out(PIECES - 1))
    forward_early(PIECES - 1)
    help_even(PIECES - 1)
    pl.when(core == 0)(lambda: relay(0))

    def forward_late():
        for k in range(PIECES):
            forward(k)

    def receive(slot):
        for k in range(PIECES):
            remote(
                piece(slot, k, zhi), piece(slot, k, zhi), x_send.at[0, k], x_recv.at[slot - 1, k], ahead(1)
            ).wait_recv()

    first_chip = x_index == 0
    second = 2 - core
    third = jnp.where(first_chip, 3, 1 + core)
    fourth = jnp.where(first_chip, 1 + core, 3)
    pl.when(first_chip & (core == 0))(forward_late)
    pl.when(core == 1)(lambda: receive(1))
    cross(second, 0, PAIRS)
    lags(second)
    relay(jnp.where(core == 0, second, 0))
    pl.when(first_chip)(lambda: receive(3))
    pl.when(jnp.logical_not(first_chip) & (core == 0))(lambda: receive(1))
    cross(third, 0, PAIRS)
    lags(third)
    pl.when(core == 1)(lambda: relay(1))
    pl.when(first_chip & (core == 1))(forward_late)
    pl.when(first_chip & (core == 0))(lambda: receive(1))
    pl.when(jnp.logical_not(first_chip))(lambda: receive(3))
    cross(fourth, 0, PAIRS)
    lags(fourth)
    relay(third)
    finish(0)
    finish(second)
    relay(fourth)
    finish(third)
    finish(fourth)

    for k in range(len(ACROSS)):
        z_copy(k).wait_send()
    halo_copy(True).wait_send()
    halo_copy(False).wait_send()
    for copy in flag_copies:
        copy.wait_send()
    for k in range(PIECES):
        detoured = last_odd | last_even if EVEN_BY[k] else last_odd
        helping = helper | even_helper(k) if EVEN_BY[k] else helper
        pl.when(jnp.logical_not(detoured))(to_next(k).wait_send)
        pl.when(detoured | helping | jumper)(detour_in(k).wait_send)
        pl.when(jnp.logical_not(last_odd))(to_sibling(k).wait_send)
        pass_up(k).wait_send()
    for r in range(ROUNDS):
        for n in range(len(PARTS)):
            y_copy(r, n).wait_send()


def on_device(spectra, valid):
    groups = spectra.reshape(5, 4, BAND, 2, CH)
    raw = jnp.transpose(groups, (2, 0, 3, 1, 4)).reshape(BAND_ROWS, CH)
    dma = pltpu.SemaphoreType.DMA
    bf16, f32 = jnp.bfloat16, jnp.float32
    out = pl.pallas_call(
        kernel,
        out_shape=jax.ShapeDtypeStruct((ROUNDS, LAGS * OWN_ROWS, CH), f32),
        in_specs=[pl.BlockSpec(memory_space=pl.ANY)] * 2,
        out_specs=pl.BlockSpec(memory_space=pltpu.VMEM),
        scratch_shapes=[
            pltpu.VMEM((GROUP_ROWS + 2 * HALO, CH), bf16),
            pltpu.VMEM((GROUP_ROWS + 2 * HALO, CH), f32),
            pltpu.VMEM((ROUNDS, FLAG_ROWS + GROUP_ROWS, CH), bf16),
            pltpu.VMEM((GROUP // 2, 2 * CH, CH), bf16),
            pltpu.VMEM((ROUNDS, HALF, CH), f32),
            pltpu.VMEM((HALF * STRIDE, CH), f32),
            pltpu.VMEM((ROUNDS, LAG_STORE * HALF, CH), f32),
            pltpu.VMEM((ROUNDS, 3, LAGS * OWN_ROWS, CH), bf16),
            pltpu.VMEM((ROUNDS, 3, LAGS * OWN_ROWS, CH), bf16),
            pltpu.VMEM((GROUP_ROWS, CH), bf16),
            pltpu.VMEM((W, CH), jnp.int32),
            pltpu.VMEM((FLAG_ROWS, CH), f32),
            pltpu.VMEM((LAG_PAD, STRIDE), bf16),
            dma((2,)), pltpu.SemaphoreType.REGULAR, dma((len(ACROSS),)), dma((len(ACROSS),)), dma((2,)), dma((2,)), dma((3,)), dma((3,)),
            dma((3, PIECES)), dma((3, PIECES)), dma((PIECES,)), dma((PIECES,)), dma((ROUNDS, 6)), dma((ROUNDS, 6)),
        ],
        compiler_params=pltpu.CompilerParams(
            collective_id=0, has_side_effects=True, vmem_limit_bytes=48 << 20
        ),
        name="correlate",
    )(raw, valid)
    return out.reshape(ROUNDS, 1, LAGS, OWN_ROWS, CH)


def solution(mesh):
    return jax.shard_map(
        on_device,
        mesh=mesh,
        in_specs=(P(None, "freq", None, "chan"), P(None, "chan")),
        out_specs=P(None, "chan", None, "freq", None),
        check_vma=False,
    )
```

```python
import functools
import math

import jax
import jax.numpy as jnp
from jax import lax
from jax.experimental import pallas as pl
from jax.experimental.pallas import tpu as pltpu
from jax.sharding import PartitionSpec as P

W = 20
BINS = 272
CH = 128
LAGS = 51
ROUNDS = 4
SMOOTH = 4
BLOCKS = 64

BAND = 34
GROUP = 68
PAIRS = GROUP // 2
ROWS = 2 * W
PAIR = 2 * ROWS
HALO = SMOOTH * ROWS
BAND_ROWS = BAND * ROWS
GROUP_ROWS = GROUP * ROWS
FLAG_ROWS = 48
STRIDE = 2 * GROUP
LAG_STORE = 56
LAG_PAD = 64
OWN_ROWS = 16
HALF = 64
CUT = 26 * OWN_ROWS
FULL = LAGS * OWN_ROWS
ACROSS = ((0, 2), (12, 5), (8, 4), (4, 4), (2, 2))
WHITEN = ((2, 13), (0, 2), (15, 5), (20, 4), (24, 4), (28, 6))
PIECES = len(WHITEN)
LEFT = ((0, 2, 2, 2, 3, 3), (1, 2, 2, 3, 2, 3))
TURN = 1

water_level = 0.5
first_bin = 30.0
period = 600.0
MESH = pl.DeviceIdType.MESH


def roll4(x):
    return pltpu.roll(x, 4, axis=1)


def loop(count, body):
    lax.fori_loop(0, count, lambda n, carry: (body(n), carry)[1], 0, unroll=unrolled(count))


def unrolled(count):
    return max(n for n in range(1, 18) if count % n == 0)


def kernel(
    raw, usable, out,
    band, mag, white, lhs, inverse, spread, lagged, outbox, inbox, detour, flags_in, flags, table,
    load_sem, go_sem, z_send, z_recv, h_send, h_recv, f_send, f_recv, x_send, x_recv, w_send, w_recv, y_send, y_recv,
):
    i, j = lax.axis_index("chan"), lax.axis_index("freq")
    y, zhi = j // 2, j % 2
    core = i % 2
    x_index = (i // 2) % 4
    z_index = zhi * 8 + i // 8
    before = jnp.where(x_index == 0, ((z_index + 15) % 16) // 8, zhi)

    def ahead(r):
        t = i + r + BLOCKS
        flip = (t // BLOCKS + 1) % 2
        return {"chan": t % BLOCKS, "freq": j + flip * (1 - 2 * zhi)}

    def along_y(d):
        return {"chan": i, "freq": ((y + d) % 4) * 2 + zhi}

    across = {"chan": i, "freq": j + 1 - 2 * zhi}
    sibling = {"chan": i + 1 - 2 * core, "freq": j}

    def first_pair(first, pairs, origin):
        return first + origin * (PAIRS - 2 * first - pairs)

    def remote(src, dst, send, recv, device):
        return pltpu.make_async_remote_copy(
            src_ref=src, dst_ref=dst, send_sem=send, recv_sem=recv,
            device_id=device, device_id_type=MESH,
        )

    loads = [
        pltpu.make_async_copy(usable, flags_in, load_sem.at[0]),
        pltpu.make_async_copy(raw, band.at[pl.ds(HALO + zhi * BAND_ROWS, BAND_ROWS)], load_sem.at[1]),
    ]
    for load in loads:
        load.start()
    barrier = pltpu.get_barrier_semaphore()
    partners = [across] + [along_y(d) for d in (1, 3)]
    partners += [ahead(r) for r in (1, 2, 3, 4, 6, 8, -1, -2, -3, -4, -6, -8)]
    for partner in partners:
        pl.semaphore_signal(barrier, inc=1, device_id=partner, device_id_type=MESH)
    loads[0].wait()
    once = flags_in[...].astype(jnp.float32)
    for g in range(5):
        flags[8 * g : 8 * g + 4, :] = once[4 * g : 4 * g + 4, :]
        flags[8 * g + 4 : 8 * g + 8, :] = once[4 * g : 4 * g + 4, :]
    flags[ROWS:FLAG_ROWS, :] = jnp.zeros((FLAG_ROWS - ROWS, CH), jnp.float32)
    white[0, 0:FLAG_ROWS, :] = flags[...].astype(jnp.bfloat16)
    for load in loads[1:]:
        load.wait()
    pl.semaphore_wait(barrier, len(partners))

    def z_copy(k):
        first, pairs = ACROSS[k]
        here = band.at[pl.ds(HALO + first_pair(first, pairs, zhi) * PAIR, pairs * PAIR)]
        return remote(here, here, z_send.at[k], z_recv.at[k], across)

    def halo_copy(top):
        src = GROUP_ROWS if top else HALO
        dst = 0 if top else HALO + GROUP_ROWS
        k = 0 if top else 1
        return remote(
            band.at[pl.ds(src, HALO)], band.at[pl.ds(dst, HALO)],
            h_send.at[k], h_recv.at[k], along_y(1 if top else 3),
        )

    def send_halo(own):
        pl.when(zhi == own)(halo_copy(True).start)
        pl.when(zhi != own)(halo_copy(False).start)

    flag_copies = [
        remote(
            white.at[0, pl.ds(0, FLAG_ROWS)], white.at[r, pl.ds(0, FLAG_ROWS)],
            f_send.at[r - 1], f_recv.at[r - 1], ahead(r),
        )
        for r in (1, 2, 3)
    ]

    sublane = lax.broadcasted_iota(jnp.int32, (1, 8, CH), 1)
    lane = lax.broadcasted_iota(jnp.int32, (1, 8, CH), 2)
    sign = jnp.where(sublane < 4, -1.0, 1.0)
    first_half = (lane % 32) < 16
    valid = flags[0:ROWS, :]

    def make_table():
        lag = lax.broadcasted_iota(jnp.int32, (LAG_PAD, STRIDE), 0)
        column = lax.broadcasted_iota(jnp.int32, (LAG_PAD, STRIDE), 1)
        bins = y * GROUP + jnp.where(column < GROUP, column, column - GROUP)
        lag_index = lag.astype(jnp.float32) - float(LAGS // 2)
        bin_freq = first_bin + bins.astype(jnp.float32)
        phase_angle = 2.0 * math.pi * lag_index * bin_freq / period
        both = jnp.where(column < GROUP, jnp.cos(phase_angle), -jnp.sin(phase_angle))
        table[...] = jnp.where(lag < LAGS, both, 0.0).astype(jnp.bfloat16)

    def magnitudes(row, pairs):
        def body(p):
            at = pl.multiple_of(row + p * PAIR, 16)
            v = band[pl.ds(at, PAIR), :].astype(jnp.float32).reshape(10, 8, CH)
            square = v * v
            m = jnp.sqrt(square + roll4(square))
            mag[pl.ds(at, PAIR), :] = m.reshape(PAIR, CH)

        loop(pairs, body)

    def whiten(start, pairs):
        def body(p):
            pair = start + p
            row = pl.multiple_of(pair * PAIR, 16)
            m = [mag[pl.ds(pl.multiple_of(row + t * ROWS, 8), ROWS), :] for t in range(10)]
            inner = ((m[1] + m[2]) + (m[3] + m[4])) + ((m[5] + m[6]) + (m[7] + m[8]))
            outs = []
            for t in range(2):
                bin_index = y * GROUP + 2 * pair + t
                count = (
                    jnp.minimum(bin_index + SMOOTH, BINS - 1) - jnp.maximum(bin_index - SMOOTH, 0) + 1
                ).astype(jnp.float32)
                total = inner + (m[0] if t == 0 else m[9])
                water = jnp.maximum(total / jnp.full((1, CH), count, jnp.float32), water_level)
                outs.append(valid / water)
            factor = jnp.concatenate(outs, axis=0)
            v = band[pl.ds(pl.multiple_of(row + HALO, 16), PAIR), :].astype(jnp.float32)
            w = (v * factor).astype(jnp.bfloat16)
            white[0, pl.ds(pl.multiple_of(FLAG_ROWS + row, 16), PAIR), :] = w
            a1 = pltpu.roll(w.astype(jnp.float32).reshape(10, 8, CH), 112 * zhi, axis=2)
            a2 = pltpu.roll(roll4(a1) * sign, 16, axis=2)
            both = jnp.where(first_half, a1, a2).reshape(PAIR, CH)
            turned = jnp.transpose(both)
            column = lax.broadcasted_iota(jnp.int32, (CH, PAIR), 1)
            lhs[pair, 0:CH, 0:PAIR] = jnp.where(column < ROWS, turned, 0.0).astype(jnp.bfloat16)
            lhs[pair, CH : 2 * CH, 0:PAIR] = jnp.where(column < ROWS, 0.0, turned).astype(jnp.bfloat16)

        loop(pairs, body)

    def cross(r, start, pairs):
        def body(p):
            pair = start + p
            rhs = white[r, pl.ds(pl.multiple_of(FLAG_ROWS + pair * PAIR, 16), PAIR), :]
            c = jnp.dot(lhs[pair, :, 0:PAIR], rhs, preferred_element_type=jnp.float32)
            for g in range(4):
                scale = inverse[r, g * 16 : (g + 1) * 16, :]
                for t in range(2):
                    for part in range(2):
                        at = t * CH + g * 32 + part * 16
                        row = g * 16 * STRIDE + part * GROUP + 2 * pair + t
                        spread[pl.ds(row, 16, stride=STRIDE), :] = c[at : at + 16, :] * scale

        loop(pairs, body)

    def usable_pairs(r):
        mine = white[0, 0:FLAG_ROWS, :].astype(jnp.float32)
        mine = pltpu.roll(mine, 112 * zhi, axis=1)
        n = jnp.dot(
            jnp.transpose(mine).astype(jnp.bfloat16), white[r, 0:FLAG_ROWS, :],
            preferred_element_type=jnp.float32,
        )
        scale = 1.0 / jnp.maximum(n * 0.5, 1.0)
        for g in range(4):
            inverse[r, g * 16 : (g + 1) * 16, :] = scale[g * 32 : g * 32 + 16, :]

    def lag_sums(r, to):
        tab = table[...]

        def body(p):
            a = OWN_ROWS * to + 2 * p
            s0 = spread[pl.ds(pl.multiple_of(a * STRIDE, 8), STRIDE), :].astype(jnp.bfloat16)
            s1 = spread[pl.ds(pl.multiple_of((a + 1) * STRIDE, 8), STRIDE), :].astype(jnp.bfloat16)
            both = jnp.concatenate([s0, s1], axis=1)
            c = jnp.dot(tab, both, preferred_element_type=jnp.float32)
            lagged[r, pl.ds(a, LAG_STORE, stride=HALF), :] = c[0:LAG_STORE, 0:CH]
            lagged[r, pl.ds(a + 1, LAG_STORE, stride=HALF), :] = c[0:LAG_STORE, CH : 2 * CH]

        loop(OWN_ROWS // 2, body)

    PARTS = ((2, 0, 1), (2, CUT, 3), (1, CUT, 1), (3, 0, 3), (1, 0, 1), (3, CUT, 3))

    def y_copy(r, n):
        d, row, way = PARTS[n]
        part = pl.ds(row, CUT if row == 0 else FULL - CUT)
        return remote(
            outbox.at[r, d - 1, part], inbox.at[r, d - 1, part], y_send.at[r, n], y_recv.at[r, n], along_y(way)
        )

    def pack_round(r, n):
        d, row, _ = PARTS[n]
        to = (y + d) % 4

        def body(l):
            at = pl.multiple_of(row + l * OWN_ROWS, 16)
            from_row = pl.multiple_of(row // OWN_ROWS * HALF + l * HALF + to * OWN_ROWS, 16)
            sums = lagged[r, pl.ds(from_row, OWN_ROWS), :]
            if n >= 4:
                sums = sums + inbox[r, 1, pl.ds(at, OWN_ROWS), :].astype(jnp.float32)
            outbox[r, d - 1, pl.ds(at, OWN_ROWS), :] = sums.astype(jnp.bfloat16)

        loop((CUT if row == 0 else FULL - CUT) // OWN_ROWS, body)

    def lags(r):
        lag_sums(r, (y + 2) % 4)
        for n in (0, 1):
            pack_round(r, n)
            y_copy(r, n).start()
        for n in (2, 3):
            lag_sums(r, (y + PARTS[n][0]) % 4)
            pack_round(r, n)
            y_copy(r, n).start()
        lag_sums(r, y)

    def relay(r):
        for n in (0, 1):
            y_copy(r, n).wait_recv()
            pack_round(r, 4 + n)
            y_copy(r, 4 + n).start()

    def total_round(r):
        def body(l):
            at = pl.multiple_of(l * OWN_ROWS, 16)
            mine = lagged[r, pl.ds(pl.multiple_of(l * HALF + y * OWN_ROWS, 16), OWN_ROWS), :]
            got = [inbox[r, d, pl.ds(at, OWN_ROWS), :].astype(jnp.float32) for d in (0, 2)]
            out[r, pl.ds(at, OWN_ROWS), :] = mine + (got[0] + got[1])

        loop(LAGS, body)

    def finish(r):
        for n in (2, 3, 4, 5):
            y_copy(r, n).wait_recv()
        total_round(r)

    def piece(slot, k, origin):
        first, pairs = WHITEN[k]
        return white.at[slot, pl.ds(FLAG_ROWS + first_pair(first, pairs, origin) * PAIR, pairs * PAIR)]

    def to_sibling(k):
        return remote(piece(0, k, zhi), piece(1, k, zhi), x_send.at[0, k], x_recv.at[0, k], ahead(1))

    def to_next(k):
        return remote(piece(0, k, zhi), piece(2, k, zhi), x_send.at[1, k], x_recv.at[1, k], ahead(2))

    def pass_up(k):
        return remote(piece(2, k, before), piece(3, k, before), x_send.at[2, k], x_recv.at[2, k], ahead(1))

    def pass_down(k):
        return remote(piece(2, k, before), piece(1, k, before), x_send.at[2, k], x_recv.at[0, k], ahead(-1))

    def pass_on(k):
        return remote(piece(2, k, before), piece(3, k, before), x_send.at[0, k], x_recv.at[2, k], ahead(1))

    def detour_rows(k):
        first, pairs = WHITEN[k]
        return detour.at[pl.ds(first_pair(first, pairs, zhi) * PAIR, pairs * PAIR)]

    def detour_in(k, chips):
        return remote(piece(0, k, zhi), detour_rows(k), w_send.at[k], w_recv.at[k], ahead(-2 * chips))

    def detour_out(k, chips):
        return remote(detour_rows(k), piece(2, k, zhi), w_send.at[k], x_recv.at[1, k], ahead(2 + 2 * chips))

    last_chip = x_index == 3
    last_odd = last_chip & (core == 1)

    def helping(side, k):
        return (core == side) & (x_index == 3 - LEFT[side][k]) & (x_index != 3)

    def help_out(side, k):
        if LEFT[side][k]:
            @pl.when(helping(side, k))
            def _():
                detour_in(k, LEFT[side][k]).wait_recv()
                detour_out(k, LEFT[side][k]).start()

    def send_own(k):
        pl.when(core == 0)(to_sibling(k).start)
        pl.when(x_index != 3)(to_next(k).start)
        for side in (0, 1):
            chips = LEFT[side][k]
            pl.when(last_chip & (core == side))(detour_in(k, chips).start if chips else to_next(k).start)

    def go_on():
        pl.semaphore_signal(go_sem, inc=1, device_id=sibling, device_id_type=MESH)

    def forward(k):
        to_next(k).wait_recv()
        pl.when(core == 0)(pass_up(k).start)
        pl.when(core == 1)(pass_down(k).start)
        pl.when((core == 1) & (x_index != 3))(pass_on(k).start)

    def forward_early(k):
        @pl.when(x_index != 0)
        def _():
            forward(k)

    def whiten_piece(k):
        first, pairs = WHITEN[k]
        whiten(first_pair(first, pairs, zhi), pairs)
        send_own(k)

    def cross_piece(k):
        first, pairs = WHITEN[k]
        cross(0, first_pair(first, pairs, zhi), pairs)

    def receive_across(k):
        z_copy(k).wait_recv()
        if k == 0:
            send_halo(0)
        first, pairs = ACROSS[k]
        magnitudes(HALO + first_pair(first, pairs, 1 - zhi) * PAIR, pairs)

    z_copy(0).start()

    @pl.when(core == 0)
    def _():
        for k in range(1, len(ACROSS)):
            z_copy(k).start()

    send_halo(1)
    for copy in flag_copies:
        copy.start()
    magnitudes(HALO + zhi * BAND_ROWS, BAND // 2)
    whiten_piece(0)
    make_table()
    usable_pairs(0)
    receive_across(0)
    cross_piece(0)
    halo_copy(True).wait_recv()
    halo_copy(False).wait_recv()
    magnitudes(0, SMOOTH // 2)
    magnitudes(HALO + GROUP_ROWS, SMOOTH // 2)

    @pl.when(y == 0)
    def _():
        mag[0:HALO, :] = jnp.zeros((HALO, CH), jnp.float32)

    @pl.when(y == 3)
    def _():
        mag[HALO + GROUP_ROWS :, :] = jnp.zeros((HALO, CH), jnp.float32)

    whiten_piece(1)
    cross_piece(1)

    @pl.when(core == 1)
    def _():
        pl.semaphore_wait(go_sem, 1)
        for k in range(1, len(ACROSS)):
            z_copy(k).start()

    for k in range(2, PIECES):
        receive_across(k - 1)
        if k - 1 == TURN:
            pl.when(core == 0)(go_on)
        whiten_piece(k)
        forward_early(k - 2)
        help_out(0, k - 2)
        help_out(1, k - 2)
        if k >= 4:
            pl.when(x_index == 0)(functools.partial(forward, k - 4))
        if k < PIECES - 1:
            cross_piece(k)
        if k == 3:
            for r in (1, 2, 3):
                flag_copies[r - 1].wait_recv()
                usable_pairs(r)

    help_out(1, PIECES - 2)

    @pl.when(last_odd)
    def _():
        for k in range(PIECES - 2):
            pass_on(k).start()

    forward_early(PIECES - 2)
    pl.when(last_odd)(pass_on(PIECES - 2).start)
    help_out(0, PIECES - 2)
    cross_piece(PIECES - 1)
    lags(0)
    help_out(1, PIECES - 1)
    forward_early(PIECES - 1)
    pl.when(last_odd)(pass_on(PIECES - 1).start)
    help_out(0, PIECES - 1)
    pl.when(core == 0)(lambda: relay(0))

    def forward_late(*pieces):
        for k in pieces:
            forward(k)

    def receive(slot):
        for k in range(PIECES):
            remote(
                piece(slot, k, zhi), piece(slot, k, zhi), x_send.at[0, k], x_recv.at[slot - 1, k], ahead(1)
            ).wait_recv()

    first_chip = x_index == 0
    second = 2 - core
    third = jnp.where(first_chip, 3, 1 + core)
    fourth = jnp.where(first_chip, 1 + core, 3)
    pl.when(first_chip)(lambda: forward_late(2, 3))
    pl.when(first_chip & (core == 0))(lambda: forward_late(4, 5))
    pl.when(core == 1)(lambda: receive(1))
    cross(second, 0, PAIRS)
    lags(second)
    relay(jnp.where(core == 0, second, 0))
    pl.when(first_chip & (core == 1))(lambda: forward_late(4, 5))
    pl.when(first_chip)(lambda: receive(3))
    pl.when(jnp.logical_not(first_chip) & (core == 0))(lambda: receive(1))
    cross(third, 0, PAIRS)
    lags(third)
    pl.when(core == 1)(lambda: relay(1))
    pl.when(first_chip & (core == 0))(lambda: receive(1))
    pl.when(jnp.logical_not(first_chip))(lambda: receive(3))
    cross(fourth, 0, PAIRS)
    lags(fourth)
    relay(third)
    finish(0)
    finish(second)
    relay(fourth)
    finish(third)
    finish(fourth)

    for k in range(len(ACROSS)):
        z_copy(k).wait_send()
    halo_copy(True).wait_send()
    halo_copy(False).wait_send()
    for copy in flag_copies:
        copy.wait_send()
    for k in range(PIECES):
        detoured, helper = last_chip & (core == 2), core == 2
        for side in (0, 1):
            if LEFT[side][k]:
                detoured = detoured | (last_chip & (core == side))
                helper = helper | helping(side, k)
        pl.when(jnp.logical_not(detoured))(to_next(k).wait_send)
        pl.when(detoured | helper)(detour_in(k, 2).wait_send)
        to_sibling(k).wait_send()
        pass_up(k).wait_send()
    for r in range(ROUNDS):
        for n in range(len(PARTS)):
            y_copy(r, n).wait_send()


def on_device(spectra, valid):
    groups = spectra.reshape(5, 4, BAND, 2, CH)
    raw = jnp.transpose(groups, (2, 0, 3, 1, 4)).reshape(BAND_ROWS, CH)
    dma = pltpu.SemaphoreType.DMA
    bf16, f32 = jnp.bfloat16, jnp.float32
    out = pl.pallas_call(
        kernel,
        out_shape=jax.ShapeDtypeStruct((ROUNDS, LAGS * OWN_ROWS, CH), f32),
        in_specs=[pl.BlockSpec(memory_space=pl.ANY)] * 2,
        out_specs=pl.BlockSpec(memory_space=pltpu.VMEM),
        scratch_shapes=[
            pltpu.VMEM((GROUP_ROWS + 2 * HALO, CH), bf16),
            pltpu.VMEM((GROUP_ROWS + 2 * HALO, CH), f32),
            pltpu.VMEM((ROUNDS, FLAG_ROWS + GROUP_ROWS, CH), bf16),
            pltpu.VMEM((GROUP // 2, 2 * CH, CH), bf16),
            pltpu.VMEM((ROUNDS, HALF, CH), f32),
            pltpu.VMEM((HALF * STRIDE, CH), f32),
            pltpu.VMEM((ROUNDS, LAG_STORE * HALF, CH), f32),
            pltpu.VMEM((ROUNDS, 3, LAGS * OWN_ROWS, CH), bf16),
            pltpu.VMEM((ROUNDS, 3, LAGS * OWN_ROWS, CH), bf16),
            pltpu.VMEM((GROUP_ROWS, CH), bf16),
            pltpu.VMEM((W, CH), jnp.int32),
            pltpu.VMEM((FLAG_ROWS, CH), f32),
            pltpu.VMEM((LAG_PAD, STRIDE), bf16),
            dma((2,)), pltpu.SemaphoreType.REGULAR, dma((len(ACROSS),)), dma((len(ACROSS),)), dma((2,)), dma((2,)), dma((3,)), dma((3,)),
            dma((3, PIECES)), dma((3, PIECES)), dma((PIECES,)), dma((PIECES,)), dma((ROUNDS, 6)), dma((ROUNDS, 6)),
        ],
        compiler_params=pltpu.CompilerParams(
            collective_id=0, has_side_effects=True, vmem_limit_bytes=48 << 20
        ),
        name="correlate",
    )(raw, valid)
    return out.reshape(ROUNDS, 1, LAGS, OWN_ROWS, CH)


def solution(mesh):
    return jax.shard_map(
        on_device,
        mesh=mesh,
        in_specs=(P(None, "freq", None, "chan"), P(None, "chan")),
        out_specs=P(None, "chan", None, "freq", None),
        check_vma=False,
    )
```

```python
import functools
import math

import jax
import jax.numpy as jnp
from jax import lax
from jax.experimental import pallas as pl
from jax.experimental.pallas import tpu as pltpu
from jax.sharding import PartitionSpec as P

W = 20
BINS = 272
CH = 128
LAGS = 51
ROUNDS = 4
SMOOTH = 4
BLOCKS = 64

BAND = 34
GROUP = 68
PAIRS = GROUP // 2
ROWS = 2 * W
PAIR = 2 * ROWS
HALO = SMOOTH * ROWS
BAND_ROWS = BAND * ROWS
GROUP_ROWS = GROUP * ROWS
FLAG_ROWS = 48
STRIDE = 2 * GROUP
LAG_STORE = 56
LAG_PAD = 64
OWN_ROWS = 16
HALF = 64
CUT = 26 * OWN_ROWS
FULL = LAGS * OWN_ROWS
ACROSS = ((0, 2), (12, 5), (8, 4), (3, 5), (2, 1))
WHITEN = ((2, 13), (0, 2), (15, 5), (20, 4), (24, 5), (29, 5))
PIECES = len(WHITEN)
LEFT = ((0, 2, 1, 2, 3, 0), (1, 2, 2, 3, 1, 0))
TURN = 1

water_level = 0.5
first_bin = 30.0
period = 600.0
MESH = pl.DeviceIdType.MESH


def roll4(x):
    return pltpu.roll(x, 4, axis=1)


def loop(count, body):
    lax.fori_loop(0, count, lambda n, carry: (body(n), carry)[1], 0, unroll=unrolled(count))


def unrolled(count):
    return max(n for n in range(1, 18) if count % n == 0)


def kernel(
    raw, usable, out,
    band, mag, white, lhs, inverse, spread, lagged, outbox, inbox, detour, flags_in, flags, table,
    load_sem, go_sem, z_send, z_recv, h_send, h_recv, f_send, f_recv, x_send, x_recv, w_send, w_recv, y_send, y_recv,
):
    i, j = lax.axis_index("chan"), lax.axis_index("freq")
    y, zhi = j // 2, j % 2
    core = i % 2
    x_index = (i // 2) % 4
    z_index = zhi * 8 + i // 8
    before = jnp.where(x_index == 0, ((z_index + 15) % 16) // 8, zhi)

    def ahead(r):
        t = i + r + BLOCKS
        flip = (t // BLOCKS + 1) % 2
        return {"chan": t % BLOCKS, "freq": j + flip * (1 - 2 * zhi)}

    def along_y(d):
        return {"chan": i, "freq": ((y + d) % 4) * 2 + zhi}

    across = {"chan": i, "freq": j + 1 - 2 * zhi}
    sibling = {"chan": i + 1 - 2 * core, "freq": j}

    def first_pair(first, pairs, origin):
        return first + origin * (PAIRS - 2 * first - pairs)

    def remote(src, dst, send, recv, device):
        return pltpu.make_async_remote_copy(
            src_ref=src, dst_ref=dst, send_sem=send, recv_sem=recv,
            device_id=device, device_id_type=MESH,
        )

    loads = [
        pltpu.make_async_copy(usable, flags_in, load_sem.at[0]),
        pltpu.make_async_copy(raw, band.at[pl.ds(HALO + zhi * BAND_ROWS, BAND_ROWS)], load_sem.at[1]),
    ]
    for load in loads:
        load.start()
    barrier = pltpu.get_barrier_semaphore()
    partners = [across] + [along_y(d) for d in (1, 3)]
    partners += [ahead(r) for r in (1, 2, 3, 4, 6, 8, -1, -2, -3, -4, -6, -8)]
    for partner in partners:
        pl.semaphore_signal(barrier, inc=1, device_id=partner, device_id_type=MESH)
    pl.semaphore_wait(barrier, len(partners))

    def z_copy(k):
        first, pairs = ACROSS[k]
        own = first + zhi * (PAIRS // 2 - 2 * first - pairs)
        return remote(
            raw.at[pl.ds(own * PAIR, pairs * PAIR)],
            band.at[pl.ds(HALO + zhi * BAND_ROWS + own * PAIR, pairs * PAIR)],
            z_send.at[k], z_recv.at[k], across,
        )

    z_copy(0).start()

    @pl.when(core == 0)
    def _():
        for k in range(1, len(ACROSS)):
            z_copy(k).start()

    loads[0].wait()
    once = flags_in[...].astype(jnp.float32)
    for g in range(5):
        flags[8 * g : 8 * g + 4, :] = once[4 * g : 4 * g + 4, :]
        flags[8 * g + 4 : 8 * g + 8, :] = once[4 * g : 4 * g + 4, :]
    flags[ROWS:FLAG_ROWS, :] = jnp.zeros((FLAG_ROWS - ROWS, CH), jnp.float32)
    white[0, 0:FLAG_ROWS, :] = flags[...].astype(jnp.bfloat16)
    for load in loads[1:]:
        load.wait()

    def halo_copy(top):
        src = GROUP_ROWS if top else HALO
        dst = 0 if top else HALO + GROUP_ROWS
        k = 0 if top else 1
        return remote(
            band.at[pl.ds(src, HALO)], band.at[pl.ds(dst, HALO)],
            h_send.at[k], h_recv.at[k], along_y(1 if top else 3),
        )

    def send_halo(own):
        pl.when(zhi == own)(halo_copy(True).start)
        pl.when(zhi != own)(halo_copy(False).start)

    flag_copies = [
        remote(
            white.at[0, pl.ds(0, FLAG_ROWS)], white.at[r, pl.ds(0, FLAG_ROWS)],
            f_send.at[r - 1], f_recv.at[r - 1], ahead(r),
        )
        for r in (1, 2, 3)
    ]

    sublane = lax.broadcasted_iota(jnp.int32, (1, 8, CH), 1)
    lane = lax.broadcasted_iota(jnp.int32, (1, 8, CH), 2)
    sign = jnp.where(sublane < 4, -1.0, 1.0)
    first_half = (lane % 32) < 16
    valid = flags[0:ROWS, :]

    def make_table():
        lag = lax.broadcasted_iota(jnp.int32, (LAG_PAD, STRIDE), 0)
        column = lax.broadcasted_iota(jnp.int32, (LAG_PAD, STRIDE), 1)
        bins = y * GROUP + jnp.where(column < GROUP, column, column - GROUP)
        lag_index = lag.astype(jnp.float32) - float(LAGS // 2)
        bin_freq = first_bin + bins.astype(jnp.float32)
        phase_angle = 2.0 * math.pi * lag_index * bin_freq / period
        both = jnp.where(column < GROUP, jnp.cos(phase_angle), -jnp.sin(phase_angle))
        table[...] = jnp.where(lag < LAGS, both, 0.0).astype(jnp.bfloat16)

    def magnitudes(row, pairs):
        def body(p):
            at = pl.multiple_of(row + p * PAIR, 16)
            v = band[pl.ds(at, PAIR), :].astype(jnp.float32).reshape(10, 8, CH)
            square = v * v
            m = jnp.sqrt(square + roll4(square))
            mag[pl.ds(at, PAIR), :] = m.reshape(PAIR, CH)

        loop(pairs, body)

    def whiten(start, pairs):
        def body(p):
            pair = start + p
            row = pl.multiple_of(pair * PAIR, 16)
            m = [mag[pl.ds(pl.multiple_of(row + t * ROWS, 8), ROWS), :] for t in range(10)]
            inner = ((m[1] + m[2]) + (m[3] + m[4])) + ((m[5] + m[6]) + (m[7] + m[8]))
            outs = []
            for t in range(2):
                bin_index = y * GROUP + 2 * pair + t
                count = (
                    jnp.minimum(bin_index + SMOOTH, BINS - 1) - jnp.maximum(bin_index - SMOOTH, 0) + 1
                ).astype(jnp.float32)
                total = inner + (m[0] if t == 0 else m[9])
                water = jnp.maximum(total / jnp.full((1, CH), count, jnp.float32), water_level)
                outs.append(valid / water)
            factor = jnp.concatenate(outs, axis=0)
            v = band[pl.ds(pl.multiple_of(row + HALO, 16), PAIR), :].astype(jnp.float32)
            w = (v * factor).astype(jnp.bfloat16)
            white[0, pl.ds(pl.multiple_of(FLAG_ROWS + row, 16), PAIR), :] = w
            a1 = pltpu.roll(w.astype(jnp.float32).reshape(10, 8, CH), 112 * zhi, axis=2)
            a2 = pltpu.roll(roll4(a1) * sign, 16, axis=2)
            both = jnp.where(first_half, a1, a2).reshape(PAIR, CH)
            turned = jnp.transpose(both)
            column = lax.broadcasted_iota(jnp.int32, (CH, PAIR), 1)
            lhs[pair, 0:CH, 0:PAIR] = jnp.where(column < ROWS, turned, 0.0).astype(jnp.bfloat16)
            lhs[pair, CH : 2 * CH, 0:PAIR] = jnp.where(column < ROWS, 0.0, turned).astype(jnp.bfloat16)

        loop(pairs, body)

    def cross(r, start, pairs):
        def body(p):
            pair = start + p
            rhs = white[r, pl.ds(pl.multiple_of(FLAG_ROWS + pair * PAIR, 16), PAIR), :]
            c = jnp.dot(lhs[pair, :, 0:PAIR], rhs, preferred_element_type=jnp.float32)
            for g in range(4):
                scale = inverse[r, g * 16 : (g + 1) * 16, :]
                for t in range(2):
                    for part in range(2):
                        at = t * CH + g * 32 + part * 16
                        row = g * 16 * STRIDE + part * GROUP + 2 * pair + t
                        spread[pl.ds(row, 16, stride=STRIDE), :] = c[at : at + 16, :] * scale

        loop(pairs, body)

    def usable_pairs(r):
        mine = white[0, 0:FLAG_ROWS, :].astype(jnp.float32)
        mine = pltpu.roll(mine, 112 * zhi, axis=1)
        n = jnp.dot(
            jnp.transpose(mine).astype(jnp.bfloat16), white[r, 0:FLAG_ROWS, :],
            preferred_element_type=jnp.float32,
        )
        scale = 1.0 / jnp.maximum(n * 0.5, 1.0)
        for g in range(4):
            inverse[r, g * 16 : (g + 1) * 16, :] = scale[g * 32 : g * 32 + 16, :]

    def lag_sums(r, to):
        tab = table[...]

        def body(p):
            a = OWN_ROWS * to + 2 * p
            s0 = spread[pl.ds(pl.multiple_of(a * STRIDE, 8), STRIDE), :].astype(jnp.bfloat16)
            s1 = spread[pl.ds(pl.multiple_of((a + 1) * STRIDE, 8), STRIDE), :].astype(jnp.bfloat16)
            both = jnp.concatenate([s0, s1], axis=1)
            c = jnp.dot(tab, both, preferred_element_type=jnp.float32)
            lagged[r, pl.ds(a, LAG_STORE, stride=HALF), :] = c[0:LAG_STORE, 0:CH]
            lagged[r, pl.ds(a + 1, LAG_STORE, stride=HALF), :] = c[0:LAG_STORE, CH : 2 * CH]

        loop(OWN_ROWS // 2, body)

    PARTS = ((2, 0, 1), (2, CUT, 3), (1, CUT, 1), (3, 0, 3), (1, 0, 1), (3, CUT, 3))

    def y_copy(r, n):
        d, row, way = PARTS[n]
        part = pl.ds(row, CUT if row == 0 else FULL - CUT)
        return remote(
            outbox.at[r, d - 1, part], inbox.at[r, d - 1, part], y_send.at[r, n], y_recv.at[r, n], along_y(way)
        )

    def pack_round(r, n):
        d, row, _ = PARTS[n]
        to = (y + d) % 4

        def body(l):
            at = pl.multiple_of(row + l * OWN_ROWS, 16)
            from_row = pl.multiple_of(row // OWN_ROWS * HALF + l * HALF + to * OWN_ROWS, 16)
            sums = lagged[r, pl.ds(from_row, OWN_ROWS), :]
            if n >= 4:
                sums = sums + inbox[r, 1, pl.ds(at, OWN_ROWS), :].astype(jnp.float32)
            outbox[r, d - 1, pl.ds(at, OWN_ROWS), :] = sums.astype(jnp.bfloat16)

        loop((CUT if row == 0 else FULL - CUT) // OWN_ROWS, body)

    def lags(r):
        lag_sums(r, (y + 2) % 4)
        for n in (0, 1):
            pack_round(r, n)
            y_copy(r, n).start()
        for n in (2, 3):
            lag_sums(r, (y + PARTS[n][0]) % 4)
            pack_round(r, n)
            y_copy(r, n).start()
        lag_sums(r, y)

    def relay(r):
        for n in (0, 1):
            y_copy(r, n).wait_recv()
            pack_round(r, 4 + n)
            y_copy(r, 4 + n).start()

    def total_round(r):
        def body(l):
            at = pl.multiple_of(l * OWN_ROWS, 16)
            sums = lagged[r, pl.ds(pl.multiple_of(l * HALF + y * OWN_ROWS, 16), OWN_ROWS), :]
            for d in (0, 2):
                sums = sums + inbox[r, d, pl.ds(at, OWN_ROWS), :].astype(jnp.float32)
            out[r, pl.ds(at, OWN_ROWS), :] = sums

        loop(LAGS, body)

    def finish(r):
        for n in (2, 3, 4, 5):
            y_copy(r, n).wait_recv()
        total_round(r)

    def piece(slot, k, origin):
        first, pairs = WHITEN[k]
        return white.at[slot, pl.ds(FLAG_ROWS + first_pair(first, pairs, origin) * PAIR, pairs * PAIR)]

    def to_sibling(k):
        return remote(piece(0, k, zhi), piece(1, k, zhi), x_send.at[0, k], x_recv.at[0, k], ahead(1))

    def to_next(k):
        return remote(piece(0, k, zhi), piece(2, k, zhi), x_send.at[1, k], x_recv.at[1, k], ahead(2))

    def pass_up(k):
        return remote(piece(2, k, before), piece(3, k, before), x_send.at[2, k], x_recv.at[2, k], ahead(1))

    def pass_down(k):
        return remote(piece(2, k, before), piece(1, k, before), x_send.at[2, k], x_recv.at[0, k], ahead(-1))

    def pass_on(k):
        return remote(piece(2, k, before), piece(3, k, before), x_send.at[0, k], x_recv.at[2, k], ahead(1))

    def detour_rows(k):
        first, pairs = WHITEN[k]
        return detour.at[pl.ds(first_pair(first, pairs, zhi) * PAIR, pairs * PAIR)]

    def detour_in(k, chips):
        return remote(piece(0, k, zhi), detour_rows(k), w_send.at[k], w_recv.at[k], ahead(-2 * chips))

    def detour_out(k, chips):
        return remote(detour_rows(k), piece(2, k, zhi), w_send.at[k], x_recv.at[1, k], ahead(2 + 2 * chips))

    last_chip = x_index == 3
    last_odd = last_chip & (core == 1)

    def helping(side, k):
        return (core == side) & (x_index == 3 - LEFT[side][k]) & (x_index != 3)

    def help_out(side, k):
        if LEFT[side][k]:
            @pl.when(helping(side, k))
            def _():
                detour_in(k, LEFT[side][k]).wait_recv()
                detour_out(k, LEFT[side][k]).start()

    def send_own(k):
        pl.when(core == 0)(to_sibling(k).start)
        pl.when(x_index != 3)(to_next(k).start)
        for side in (0, 1):
            chips = LEFT[side][k]
            pl.when(last_chip & (core == side))(detour_in(k, chips).start if chips else to_next(k).start)

    def go_on():
        pl.semaphore_signal(go_sem, inc=1, device_id=sibling, device_id_type=MESH)

    def forward(k):
        to_next(k).wait_recv()
        pl.when(core == 0)(pass_up(k).start)
        pl.when(core == 1)(pass_down(k).start)
        pl.when((core == 1) & (x_index != 3))(pass_on(k).start)

    def forward_early(k):
        @pl.when(x_index != 0)
        def _():
            forward(k)

    def whiten_piece(k):
        first, pairs = WHITEN[k]
        whiten(first_pair(first, pairs, zhi), pairs)
        send_own(k)

    def cross_piece(k):
        first, pairs = WHITEN[k]
        cross(0, first_pair(first, pairs, zhi), pairs)

    def receive_across(k):
        z_copy(k).wait_recv()
        if k == 0:
            send_halo(0)
        first, pairs = ACROSS[k]
        magnitudes(HALO + first_pair(first, pairs, 1 - zhi) * PAIR, pairs)

    send_halo(1)
    for copy in flag_copies:
        copy.start()
    magnitudes(HALO + zhi * BAND_ROWS, BAND // 2)
    whiten_piece(0)
    make_table()
    usable_pairs(0)
    receive_across(0)
    cross_piece(0)
    halo_copy(True).wait_recv()
    halo_copy(False).wait_recv()
    magnitudes(0, SMOOTH // 2)
    magnitudes(HALO + GROUP_ROWS, SMOOTH // 2)

    @pl.when(y == 0)
    def _():
        mag[0:HALO, :] = jnp.zeros((HALO, CH), jnp.float32)

    @pl.when(y == 3)
    def _():
        mag[HALO + GROUP_ROWS :, :] = jnp.zeros((HALO, CH), jnp.float32)

    whiten_piece(1)
    cross_piece(1)

    @pl.when(core == 1)
    def _():
        pl.semaphore_wait(go_sem, 1)
        for k in range(1, len(ACROSS)):
            z_copy(k).start()

    for k in range(2, PIECES):
        receive_across(k - 1)
        if k - 1 == TURN:
            pl.when(core == 0)(go_on)
        whiten_piece(k)
        forward_early(k - 2)
        help_out(0, k - 2)
        if k == 2:
            help_out(1, 0)
        if k == 4:
            pl.when(x_index == 0)(functools.partial(forward, 0))
        if k == 5:
            pl.when(last_odd)(pass_on(0).start)
        if k < PIECES - 1:
            cross_piece(k)
        if k == 3:
            for r in (1, 2, 3):
                flag_copies[r - 1].wait_recv()
                usable_pairs(r)

    for k in range(1, PIECES - 2):
        help_out(1, k)

    @pl.when(last_odd)
    def _():
        for k in range(1, PIECES - 2):
            pass_on(k).start()

    cross_piece(PIECES - 1)
    lags(0)
    for k in (PIECES - 2, PIECES - 1):
        forward_early(k)
        pl.when(last_odd)(pass_on(k).start)
        help_out(0, k)
        help_out(1, k)
    pl.when(core == 0)(lambda: relay(0))

    def forward_late(*pieces):
        for k in pieces:
            forward(k)

    def receive(slot):
        for k in range(PIECES):
            remote(
                piece(slot, k, zhi), piece(slot, k, zhi), x_send.at[0, k], x_recv.at[slot - 1, k], ahead(1)
            ).wait_recv()

    first_chip = x_index == 0
    second = 2 - core
    third = jnp.where(first_chip, 3, 1 + core)
    fourth = jnp.where(first_chip, 1 + core, 3)
    pl.when(first_chip & (core == 0))(lambda: forward_late(1, 2, 3, 4, 5))
    pl.when(core == 1)(lambda: receive(1))
    cross(second, 0, PAIRS)
    lags(second)
    pl.when(first_chip & (core == 1))(lambda: forward_late(1, 2, 3, 4))
    relay(jnp.where(core == 0, second, 0))
    pl.when(first_chip)(lambda: receive(3))
    pl.when(jnp.logical_not(first_chip) & (core == 0))(lambda: receive(1))
    cross(third, 0, PAIRS)
    lags(third)
    pl.when(first_chip & (core == 1))(lambda: forward_late(5))
    pl.when(core == 1)(lambda: relay(1))
    pl.when(first_chip & (core == 0))(lambda: receive(1))
    pl.when(jnp.logical_not(first_chip))(lambda: receive(3))
    cross(fourth, 0, PAIRS)
    lags(fourth)
    relay(third)
    finish(0)
    finish(second)
    relay(fourth)
    finish(third)
    finish(fourth)

    for k in range(len(ACROSS)):
        z_copy(k).wait_send()
    halo_copy(True).wait_send()
    halo_copy(False).wait_send()
    for copy in flag_copies:
        copy.wait_send()
    for k in range(PIECES):
        detoured, helper = last_chip & (core == 2), core == 2
        for side in (0, 1):
            if LEFT[side][k]:
                detoured = detoured | (last_chip & (core == side))
                helper = helper | helping(side, k)
        pl.when(jnp.logical_not(detoured))(to_next(k).wait_send)
        pl.when(detoured | helper)(detour_in(k, 2).wait_send)
        to_sibling(k).wait_send()
        pass_up(k).wait_send()
    for r in range(ROUNDS):
        for n in range(len(PARTS)):
            y_copy(r, n).wait_send()


def on_device(spectra, valid):
    groups = spectra.reshape(5, 4, BAND, 2, CH)
    raw = jnp.transpose(groups, (2, 0, 3, 1, 4)).reshape(BAND_ROWS, CH)
    dma = pltpu.SemaphoreType.DMA
    bf16, f32 = jnp.bfloat16, jnp.float32
    out = pl.pallas_call(
        kernel,
        out_shape=jax.ShapeDtypeStruct((ROUNDS, LAGS * OWN_ROWS, CH), f32),
        in_specs=[pl.BlockSpec(memory_space=pl.ANY)] * 2,
        out_specs=pl.BlockSpec(memory_space=pltpu.VMEM),
        scratch_shapes=[
            pltpu.VMEM((GROUP_ROWS + 2 * HALO, CH), bf16),
            pltpu.VMEM((GROUP_ROWS + 2 * HALO, CH), f32),
            pltpu.VMEM((ROUNDS, FLAG_ROWS + GROUP_ROWS, CH), bf16),
            pltpu.VMEM((GROUP // 2, 2 * CH, CH), bf16),
            pltpu.VMEM((ROUNDS, HALF, CH), f32),
            pltpu.VMEM((HALF * STRIDE, CH), f32),
            pltpu.VMEM((ROUNDS, LAG_STORE * HALF, CH), f32),
            pltpu.VMEM((ROUNDS, 3, LAGS * OWN_ROWS, CH), bf16),
            pltpu.VMEM((ROUNDS, 3, LAGS * OWN_ROWS, CH), bf16),
            pltpu.VMEM((GROUP_ROWS, CH), bf16),
            pltpu.VMEM((W, CH), jnp.int32),
            pltpu.VMEM((FLAG_ROWS, CH), f32),
            pltpu.VMEM((LAG_PAD, STRIDE), bf16),
            dma((2,)), pltpu.SemaphoreType.REGULAR, dma((len(ACROSS),)), dma((len(ACROSS),)), dma((2,)), dma((2,)), dma((3,)), dma((3,)),
            dma((3, PIECES)), dma((3, PIECES)), dma((PIECES,)), dma((PIECES,)), dma((ROUNDS, 6)), dma((ROUNDS, 6)),
        ],
        compiler_params=pltpu.CompilerParams(
            collective_id=0, has_side_effects=True, vmem_limit_bytes=48 << 20
        ),
        name="correlate",
    )(raw, valid)
    return out.reshape(ROUNDS, 1, LAGS, OWN_ROWS, CH)


def solution(mesh):
    return jax.shard_map(
        on_device,
        mesh=mesh,
        in_specs=(P(None, "freq", None, "chan"), P(None, "chan")),
        out_specs=P(None, "chan", None, "freq", None),
        check_vma=False,
    )
```

```python
import functools
import math

import jax
import jax.numpy as jnp
from jax import lax
from jax.experimental import pallas as pl
from jax.experimental.pallas import tpu as pltpu
from jax.sharding import PartitionSpec as P

W = 20
BINS = 272
CH = 128
LAGS = 51
ROUNDS = 4
SMOOTH = 4
BLOCKS = 64

BAND = 34
GROUP = 68
PAIRS = GROUP // 2
ROWS = 2 * W
PAIR = 2 * ROWS
HALO = SMOOTH * ROWS
BAND_ROWS = BAND * ROWS
GROUP_ROWS = GROUP * ROWS
FLAG_ROWS = 48
STRIDE = 2 * GROUP
LAG_STORE = 56
LAG_PAD = 64
OWN_ROWS = 16
HALF = 64
CUT = 26 * OWN_ROWS
FULL = LAGS * OWN_ROWS
ACROSS = ((0, 2), (12, 5), (8, 4), (3, 5), (2, 1))
WHITEN = ((2, 13), (0, 2), (15, 5), (20, 4), (24, 5), (29, 5))
PIECES = len(WHITEN)
LEFT = ((0, 2, 1, 2, 3, 0), (1, 2, 2, 3, 1, 0))
TURN = 1

water_level = 0.5
first_bin = 30.0
period = 600.0
MESH = pl.DeviceIdType.MESH


def roll4(x):
    return pltpu.roll(x, 4, axis=1)


def loop(count, body):
    lax.fori_loop(0, count, lambda n, carry: (body(n), carry)[1], 0, unroll=unrolled(count))


def unrolled(count):
    return max(n for n in range(1, 18) if count % n == 0)


def kernel(
    raw, usable, out,
    band, mag, white, lhs, inverse, spread, lagged, outbox, inbox, detour, flags_in, flags, table,
    load_sem, go_sem, z_send, z_recv, h_send, h_recv, f_send, f_recv, x_send, x_recv, w_send, w_recv, y_send, y_recv,
):
    i, j = lax.axis_index("chan"), lax.axis_index("freq")
    y, zhi = j // 2, j % 2
    core = i % 2
    x_index = (i // 2) % 4
    z_index = zhi * 8 + i // 8
    before = jnp.where(x_index == 0, ((z_index + 15) % 16) // 8, zhi)

    def ahead(r):
        t = i + r + BLOCKS
        flip = (t // BLOCKS + 1) % 2
        return {"chan": t % BLOCKS, "freq": j + flip * (1 - 2 * zhi)}

    def along_y(d):
        return {"chan": i, "freq": ((y + d) % 4) * 2 + zhi}

    across = {"chan": i, "freq": j + 1 - 2 * zhi}
    sibling = {"chan": i + 1 - 2 * core, "freq": j}

    def first_pair(first, pairs, origin):
        return first + origin * (PAIRS - 2 * first - pairs)

    def remote(src, dst, send, recv, device):
        return pltpu.make_async_remote_copy(
            src_ref=src, dst_ref=dst, send_sem=send, recv_sem=recv,
            device_id=device, device_id_type=MESH,
        )

    loads = [
        pltpu.make_async_copy(usable, flags_in, load_sem.at[0]),
        pltpu.make_async_copy(raw, band.at[pl.ds(HALO + zhi * BAND_ROWS, BAND_ROWS)], load_sem.at[1]),
    ]
    for load in loads:
        load.start()
    barrier = pltpu.get_barrier_semaphore()
    partners = [across] + [along_y(d) for d in (1, 3)]
    partners += [ahead(r) for r in (1, 2, 3, 4, 6, 8, -1, -2, -3, -4, -6, -8)]
    for partner in partners:
        pl.semaphore_signal(barrier, inc=1, device_id=partner, device_id_type=MESH)
    pl.semaphore_wait(barrier, len(partners))

    def z_copy(k):
        first, pairs = ACROSS[k]
        own = first + zhi * (PAIRS // 2 - 2 * first - pairs)
        return remote(
            raw.at[pl.ds(own * PAIR, pairs * PAIR)],
            band.at[pl.ds(HALO + zhi * BAND_ROWS + own * PAIR, pairs * PAIR)],
            z_send.at[k], z_recv.at[k], across,
        )

    z_copy(0).start()

    @pl.when(core == 0)
    def _():
        for k in range(1, len(ACROSS)):
            z_copy(k).start()

    loads[0].wait()
    once = flags_in[...].astype(jnp.float32)
    for g in range(5):
        flags[8 * g : 8 * g + 4, :] = once[4 * g : 4 * g + 4, :]
        flags[8 * g + 4 : 8 * g + 8, :] = once[4 * g : 4 * g + 4, :]
    flags[ROWS:FLAG_ROWS, :] = jnp.zeros((FLAG_ROWS - ROWS, CH), jnp.float32)
    white[0, 0:FLAG_ROWS, :] = flags[...].astype(jnp.bfloat16)
    for load in loads[1:]:
        load.wait()

    def halo_copy(top):
        src = GROUP_ROWS if top else HALO
        dst = 0 if top else HALO + GROUP_ROWS
        k = 0 if top else 1
        return remote(
            band.at[pl.ds(src, HALO)], band.at[pl.ds(dst, HALO)],
            h_send.at[k], h_recv.at[k], along_y(1 if top else 3),
        )

    def send_halo(own):
        pl.when(zhi == own)(halo_copy(True).start)
        pl.when(zhi != own)(halo_copy(False).start)

    flag_copies = [
        remote(
            white.at[0, pl.ds(0, FLAG_ROWS)], white.at[r, pl.ds(0, FLAG_ROWS)],
            f_send.at[r - 1], f_recv.at[r - 1], ahead(r),
        )
        for r in (1, 2, 3)
    ]

    sublane = lax.broadcasted_iota(jnp.int32, (1, 8, CH), 1)
    lane = lax.broadcasted_iota(jnp.int32, (1, 8, CH), 2)
    sign = jnp.where(sublane < 4, -1.0, 1.0)
    first_half = (lane % 32) < 16
    valid = flags[0:ROWS, :]

    def make_table():
        lag = lax.broadcasted_iota(jnp.int32, (LAG_PAD, STRIDE), 0)
        column = lax.broadcasted_iota(jnp.int32, (LAG_PAD, STRIDE), 1)
        bins = y * GROUP + jnp.where(column < GROUP, column, column - GROUP)
        lag_index = lag.astype(jnp.float32) - float(LAGS // 2)
        bin_freq = first_bin + bins.astype(jnp.float32)
        phase_angle = 2.0 * math.pi * lag_index * bin_freq / period
        both = jnp.where(column < GROUP, jnp.cos(phase_angle), -jnp.sin(phase_angle))
        table[...] = jnp.where(lag < LAGS, both, 0.0).astype(jnp.bfloat16)

    def magnitudes(row, pairs):
        def body(p):
            at = pl.multiple_of(row + p * PAIR, 16)
            v = band[pl.ds(at, PAIR), :].astype(jnp.float32).reshape(10, 8, CH)
            square = v * v
            m = jnp.sqrt(square + roll4(square))
            mag[pl.ds(at, PAIR), :] = m.reshape(PAIR, CH)

        loop(pairs, body)

    def whiten(start, pairs):
        def body(p):
            pair = start + p
            row = pl.multiple_of(pair * PAIR, 16)
            m = [mag[pl.ds(pl.multiple_of(row + t * ROWS, 8), ROWS), :] for t in range(10)]
            inner = ((m[1] + m[2]) + (m[3] + m[4])) + ((m[5] + m[6]) + (m[7] + m[8]))
            outs = []
            for t in range(2):
                bin_index = y * GROUP + 2 * pair + t
                count = (
                    jnp.minimum(bin_index + SMOOTH, BINS - 1) - jnp.maximum(bin_index - SMOOTH, 0) + 1
                ).astype(jnp.float32)
                total = inner + (m[0] if t == 0 else m[9])
                water = jnp.maximum(total / jnp.full((1, CH), count, jnp.float32), water_level)
                outs.append(valid / water)
            factor = jnp.concatenate(outs, axis=0)
            v = band[pl.ds(pl.multiple_of(row + HALO, 16), PAIR), :].astype(jnp.float32)
            w = (v * factor).astype(jnp.bfloat16)
            white[0, pl.ds(pl.multiple_of(FLAG_ROWS + row, 16), PAIR), :] = w
            a1 = pltpu.roll(w.astype(jnp.float32).reshape(10, 8, CH), 112 * zhi, axis=2)
            a2 = pltpu.roll(roll4(a1) * sign, 16, axis=2)
            both = jnp.where(first_half, a1, a2).reshape(PAIR, CH)
            turned = jnp.transpose(both)
            column = lax.broadcasted_iota(jnp.int32, (CH, PAIR), 1)
            lhs[pair, 0:CH, 0:PAIR] = jnp.where(column < ROWS, turned, 0.0).astype(jnp.bfloat16)
            lhs[pair, CH : 2 * CH, 0:PAIR] = jnp.where(column < ROWS, 0.0, turned).astype(jnp.bfloat16)

        loop(pairs, body)

    def cross(r, start, pairs):
        def body(p):
            pair = start + p
            rhs = white[r, pl.ds(pl.multiple_of(FLAG_ROWS + pair * PAIR, 16), PAIR), :]
            c = jnp.dot(lhs[pair, :, 0:PAIR], rhs, preferred_element_type=jnp.float32)
            for g in range(4):
                scale = inverse[r, g * 16 : (g + 1) * 16, :]
                for t in range(2):
                    for part in range(2):
                        at = t * CH + g * 32 + part * 16
                        row = g * 16 * STRIDE + part * GROUP + 2 * pair + t
                        spread[pl.ds(row, 16, stride=STRIDE), :] = c[at : at + 16, :] * scale

        loop(pairs, body)

    def usable_pairs(r):
        mine = white[0, 0:FLAG_ROWS, :].astype(jnp.float32)
        mine = pltpu.roll(mine, 112 * zhi, axis=1)
        n = jnp.dot(
            jnp.transpose(mine).astype(jnp.bfloat16), white[r, 0:FLAG_ROWS, :],
            preferred_element_type=jnp.float32,
        )
        scale = 1.0 / jnp.maximum(n * 0.5, 1.0)
        for g in range(4):
            inverse[r, g * 16 : (g + 1) * 16, :] = scale[g * 32 : g * 32 + 16, :]

    def lag_sums(r, to):
        tab = table[...]

        def body(p):
            a = OWN_ROWS * to + 2 * p
            s0 = spread[pl.ds(pl.multiple_of(a * STRIDE, 8), STRIDE), :].astype(jnp.bfloat16)
            s1 = spread[pl.ds(pl.multiple_of((a + 1) * STRIDE, 8), STRIDE), :].astype(jnp.bfloat16)
            both = jnp.concatenate([s0, s1], axis=1)
            c = jnp.dot(tab, both, preferred_element_type=jnp.float32)
            lagged[r, pl.ds(a, LAG_STORE, stride=HALF), :] = c[0:LAG_STORE, 0:CH]
            lagged[r, pl.ds(a + 1, LAG_STORE, stride=HALF), :] = c[0:LAG_STORE, CH : 2 * CH]

        loop(OWN_ROWS // 2, body)

    PARTS = ((2, 0, 1), (2, CUT, 3), (1, CUT, 1), (3, 0, 3), (1, 0, 1), (3, CUT, 3))

    def y_copy(r, n):
        d, row, way = PARTS[n]
        part = pl.ds(row, CUT if row == 0 else FULL - CUT)
        return remote(
            outbox.at[r, d - 1, part], inbox.at[r, d - 1, part], y_send.at[r, n], y_recv.at[r, n], along_y(way)
        )

    def pack_round(r, n):
        d, row, _ = PARTS[n]
        to = (y + d) % 4

        def body(l):
            at = pl.multiple_of(row + l * OWN_ROWS, 16)
            from_row = pl.multiple_of(row // OWN_ROWS * HALF + l * HALF + to * OWN_ROWS, 16)
            sums = lagged[r, pl.ds(from_row, OWN_ROWS), :]
            if n >= 4:
                sums = sums + inbox[r, 1, pl.ds(at, OWN_ROWS), :].astype(jnp.float32)
            outbox[r, d - 1, pl.ds(at, OWN_ROWS), :] = sums.astype(jnp.bfloat16)

        loop((CUT if row == 0 else FULL - CUT) // OWN_ROWS, body)

    def lags(r):
        lag_sums(r, (y + 2) % 4)
        for n in (0, 1):
            pack_round(r, n)
            y_copy(r, n).start()
        for n in (2, 3):
            lag_sums(r, (y + PARTS[n][0]) % 4)
            pack_round(r, n)
            y_copy(r, n).start()
        lag_sums(r, y)

    def relay(r):
        for n in (0, 1):
            y_copy(r, n).wait_recv()
            pack_round(r, 4 + n)
            y_copy(r, 4 + n).start()

    def total_round(r):
        def body(l):
            at = pl.multiple_of(l * OWN_ROWS, 16)
            sums = lagged[r, pl.ds(pl.multiple_of(l * HALF + y * OWN_ROWS, 16), OWN_ROWS), :]
            for d in (0, 2):
                sums = sums + inbox[r, d, pl.ds(at, OWN_ROWS), :].astype(jnp.float32)
            out[r, pl.ds(at, OWN_ROWS), :] = sums

        loop(LAGS, body)

    def finish(r):
        for n in (2, 3, 4, 5):
            y_copy(r, n).wait_recv()
        total_round(r)

    def piece(slot, k, origin):
        first, pairs = WHITEN[k]
        return white.at[slot, pl.ds(FLAG_ROWS + first_pair(first, pairs, origin) * PAIR, pairs * PAIR)]

    def to_sibling(k):
        return remote(piece(0, k, zhi), piece(1, k, zhi), x_send.at[0, k], x_recv.at[0, k], ahead(1))

    def to_next(k):
        return remote(piece(0, k, zhi), piece(2, k, zhi), x_send.at[1, k], x_recv.at[1, k], ahead(2))

    def pass_up(k):
        return remote(piece(2, k, before), piece(3, k, before), x_send.at[2, k], x_recv.at[2, k], ahead(1))

    def pass_down(k):
        return remote(piece(2, k, before), piece(1, k, before), x_send.at[2, k], x_recv.at[0, k], ahead(-1))

    def pass_on(k):
        return remote(piece(2, k, before), piece(3, k, before), x_send.at[0, k], x_recv.at[2, k], ahead(1))

    def detour_rows(k):
        first, pairs = WHITEN[k]
        return detour.at[pl.ds(first_pair(first, pairs, zhi) * PAIR, pairs * PAIR)]

    def detour_in(k, chips):
        return remote(piece(0, k, zhi), detour_rows(k), w_send.at[k], w_recv.at[k], ahead(-2 * chips))

    def detour_out(k, chips):
        return remote(detour_rows(k), piece(2, k, zhi), w_send.at[k], x_recv.at[1, k], ahead(2 + 2 * chips))

    last_chip = x_index == 3
    last_odd = last_chip & (core == 1)

    def helping(side, k):
        return (core == side) & (x_index == 3 - LEFT[side][k]) & (x_index != 3)

    def help_out(side, k):
        if LEFT[side][k]:
            @pl.when(helping(side, k))
            def _():
                detour_in(k, LEFT[side][k]).wait_recv()
                detour_out(k, LEFT[side][k]).start()

    def send_own(k):
        pl.when(core == 0)(to_sibling(k).start)
        pl.when(x_index != 3)(to_next(k).start)
        for side in (0, 1):
            chips = LEFT[side][k]
            pl.when(last_chip & (core == side))(detour_in(k, chips).start if chips else to_next(k).start)

    def go_on():
        pl.semaphore_signal(go_sem, inc=1, device_id=sibling, device_id_type=MESH)

    def forward(k):
        to_next(k).wait_recv()
        pl.when(core == 0)(pass_up(k).start)
        pl.when(core == 1)(pass_down(k).start)
        pl.when((core == 1) & (x_index != 3))(pass_on(k).start)

    def forward_early(k):
        @pl.when(x_index != 0)
        def _():
            forward(k)

    def whiten_piece(k):
        first, pairs = WHITEN[k]
        whiten(first_pair(first, pairs, zhi), pairs)
        send_own(k)

    def cross_piece(k):
        first, pairs = WHITEN[k]
        cross(0, first_pair(first, pairs, zhi), pairs)

    def receive_across(k):
        z_copy(k).wait_recv()
        if k == 0:
            send_halo(0)
        first, pairs = ACROSS[k]
        magnitudes(HALO + first_pair(first, pairs, 1 - zhi) * PAIR, pairs)

    send_halo(1)
    for copy in flag_copies:
        copy.start()
    magnitudes(HALO + zhi * BAND_ROWS, BAND // 2)
    whiten_piece(0)
    make_table()
    usable_pairs(0)
    receive_across(0)
    cross_piece(0)
    halo_copy(True).wait_recv()
    halo_copy(False).wait_recv()
    magnitudes(0, SMOOTH // 2)
    magnitudes(HALO + GROUP_ROWS, SMOOTH // 2)

    @pl.when(y == 0)
    def _():
        mag[0:HALO, :] = jnp.zeros((HALO, CH), jnp.float32)

    @pl.when(y == 3)
    def _():
        mag[HALO + GROUP_ROWS :, :] = jnp.zeros((HALO, CH), jnp.float32)

    whiten_piece(1)
    cross_piece(1)

    @pl.when(core == 1)
    def _():
        pl.semaphore_wait(go_sem, 1)
        for k in range(1, len(ACROSS)):
            z_copy(k).start()

    for k in range(2, PIECES):
        receive_across(k - 1)
        if k - 1 == TURN:
            pl.when(core == 0)(go_on)
        whiten_piece(k)
        forward_early(k - 2)
        help_out(0, k - 2)
        if k == 2:
            help_out(1, 0)
        if k == 4:
            pl.when(x_index == 0)(functools.partial(forward, 0))
        if k == 5:
            pl.when(last_odd)(pass_on(0).start)
        if k < PIECES - 1:
            cross_piece(k)
        if k == 3:
            for r in (1, 2, 3):
                flag_copies[r - 1].wait_recv()
                usable_pairs(r)

    for k in range(1, PIECES - 2):
        help_out(1, k)

    @pl.when(last_odd)
    def _():
        for k in range(1, PIECES - 2):
            pass_on(k).start()

    cross_piece(PIECES - 1)
    lags(0)
    for k in (PIECES - 2, PIECES - 1):
        forward_early(k)
        pl.when(last_odd)(pass_on(k).start)
        help_out(0, k)
        help_out(1, k)
    pl.when(core == 0)(lambda: relay(0))

    def forward_late(*pieces):
        for k in pieces:
            forward(k)

    def receive(slot):
        for k in range(PIECES):
            remote(
                piece(slot, k, zhi), piece(slot, k, zhi), x_send.at[0, k], x_recv.at[slot - 1, k], ahead(1)
            ).wait_recv()

    first_chip = x_index == 0
    second = 2 - core
    third = jnp.where(first_chip, 3, 1 + core)
    fourth = jnp.where(first_chip, 1 + core, 3)
    pl.when(first_chip & (core == 0))(lambda: forward_late(1, 2, 3, 4, 5))
    pl.when(core == 1)(lambda: receive(1))
    cross(second, 0, PAIRS)
    lags(second)
    pl.when(first_chip & (core == 1))(lambda: forward_late(1, 2, 3, 4))
    relay(jnp.where(core == 0, second, 0))
    pl.when(first_chip)(lambda: receive(3))
    pl.when(jnp.logical_not(first_chip) & (core == 0))(lambda: receive(1))
    cross(third, 0, PAIRS)
    lags(third)
    pl.when(first_chip & (core == 1))(lambda: forward_late(5))
    pl.when(core == 1)(lambda: relay(1))
    pl.when(first_chip & (core == 0))(lambda: receive(1))
    pl.when(jnp.logical_not(first_chip))(lambda: receive(3))
    cross(fourth, 0, PAIRS)
    lags(fourth)
    relay(third)
    finish(0)
    finish(second)
    relay(fourth)
    finish(third)
    finish(fourth)

    for k in range(len(ACROSS)):
        z_copy(k).wait_send()
    halo_copy(True).wait_send()
    halo_copy(False).wait_send()
    for copy in flag_copies:
        copy.wait_send()
    for k in range(PIECES):
        detoured, helper = last_chip & (core == 2), core == 2
        for side in (0, 1):
            if LEFT[side][k]:
                detoured = detoured | (last_chip & (core == side))
                helper = helper | helping(side, k)
        pl.when(jnp.logical_not(detoured))(to_next(k).wait_send)
        pl.when(detoured | helper)(detour_in(k, 2).wait_send)
        to_sibling(k).wait_send()
        pass_up(k).wait_send()
    for r in range(ROUNDS):
        for n in range(len(PARTS)):
            y_copy(r, n).wait_send()


def on_device(spectra, valid):
    groups = spectra.reshape(5, 4, BAND, 2, CH)
    raw = jnp.transpose(groups, (2, 0, 3, 1, 4)).reshape(BAND_ROWS, CH)
    dma = pltpu.SemaphoreType.DMA
    bf16, f32 = jnp.bfloat16, jnp.float32
    out = pl.pallas_call(
        kernel,
        out_shape=jax.ShapeDtypeStruct((ROUNDS, LAGS * OWN_ROWS, CH), f32),
        in_specs=[pl.BlockSpec(memory_space=pl.ANY)] * 2,
        out_specs=pl.BlockSpec(memory_space=pltpu.VMEM),
        scratch_shapes=[
            pltpu.VMEM((GROUP_ROWS + 2 * HALO, CH), bf16),
            pltpu.VMEM((GROUP_ROWS + 2 * HALO, CH), f32),
            pltpu.VMEM((ROUNDS, FLAG_ROWS + GROUP_ROWS, CH), bf16),
            pltpu.VMEM((GROUP // 2, 2 * CH, CH), bf16),
            pltpu.VMEM((ROUNDS, HALF, CH), f32),
            pltpu.VMEM(((HALF + 1) * STRIDE, CH), f32),
            pltpu.VMEM((ROUNDS, (LAG_STORE + 1) * HALF, CH), f32),
            pltpu.VMEM((ROUNDS, 3, LAGS * OWN_ROWS, CH), bf16),
            pltpu.VMEM((ROUNDS, 3, LAGS * OWN_ROWS, CH), bf16),
            pltpu.VMEM((GROUP_ROWS, CH), bf16),
            pltpu.VMEM((W, CH), jnp.int32),
            pltpu.VMEM((FLAG_ROWS, CH), f32),
            pltpu.VMEM((LAG_PAD, STRIDE), bf16),
            dma((2,)), pltpu.SemaphoreType.REGULAR, dma((len(ACROSS),)), dma((len(ACROSS),)), dma((2,)), dma((2,)), dma((3,)), dma((3,)),
            dma((3, PIECES)), dma((3, PIECES)), dma((PIECES,)), dma((PIECES,)), dma((ROUNDS, 6)), dma((ROUNDS, 6)),
        ],
        compiler_params=pltpu.CompilerParams(
            collective_id=0, has_side_effects=True, vmem_limit_bytes=48 << 20
        ),
        name="correlate",
    )(raw, valid)
    return out.reshape(ROUNDS, 1, LAGS, OWN_ROWS, CH)


def solution(mesh):
    return jax.shard_map(
        on_device,
        mesh=mesh,
        in_specs=(P(None, "freq", None, "chan"), P(None, "chan")),
        out_specs=P(None, "chan", None, "freq", None),
        check_vma=False,
    )
```

```python
import functools
import math

import jax
import jax.numpy as jnp
from jax import lax
from jax.experimental import pallas as pl
from jax.experimental.pallas import tpu as pltpu
from jax.sharding import PartitionSpec as P

W = 20
BINS = 272
CH = 128
LAGS = 51
ROUNDS = 4
SMOOTH = 4
BLOCKS = 64

BAND = 34
GROUP = 68
PAIRS = GROUP // 2
ROWS = 2 * W
PAIR = 2 * ROWS
HALO = SMOOTH * ROWS
BAND_ROWS = BAND * ROWS
GROUP_ROWS = GROUP * ROWS
FLAG_ROWS = 48
STRIDE = 2 * GROUP
LAG_STORE = 56
LAG_PAD = 64
OWN_ROWS = 16
HALF = 64
CUT = 26 * OWN_ROWS
FULL = LAGS * OWN_ROWS
ACROSS = ((0, 2), (12, 5), (8, 4), (3, 5), (2, 1))
WHITEN = ((2, 13), (0, 2), (15, 5), (20, 4), (24, 5), (29, 5))
PIECES = len(WHITEN)
LEFT = ((0, 2, 1, 2, 3, 0), (1, 2, 2, 3, 1, 0))
TURN = 1

water_level = 0.5
first_bin = 30.0
period = 600.0
MESH = pl.DeviceIdType.MESH


def roll4(x):
    return pltpu.roll(x, 4, axis=1)


def loop(count, body):
    lax.fori_loop(0, count, lambda n, carry: (body(n), carry)[1], 0, unroll=unrolled(count))


def unrolled(count):
    return max(n for n in range(1, 18) if count % n == 0)


def kernel(
    raw, usable, out,
    band, mag, white, lhs, inverse, spread, lagged, outbox, inbox, detour, flags_in, flags, table,
    load_sem, go_sem, z_send, z_recv, h_send, h_recv, f_send, f_recv, x_send, x_recv, w_send, w_recv, y_send, y_recv,
):
    i, j = lax.axis_index("chan"), lax.axis_index("freq")
    y, zhi = j // 2, j % 2
    core = i % 2
    x_index = (i // 2) % 4
    z_index = zhi * 8 + i // 8
    before = jnp.where(x_index == 0, ((z_index + 15) % 16) // 8, zhi)

    def ahead(r):
        t = i + r + BLOCKS
        flip = (t // BLOCKS + 1) % 2
        return {"chan": t % BLOCKS, "freq": j + flip * (1 - 2 * zhi)}

    def along_y(d):
        return {"chan": i, "freq": ((y + d) % 4) * 2 + zhi}

    across = {"chan": i, "freq": j + 1 - 2 * zhi}
    sibling = {"chan": i + 1 - 2 * core, "freq": j}

    def first_pair(first, pairs, origin):
        return first + origin * (PAIRS - 2 * first - pairs)

    def remote(src, dst, send, recv, device):
        return pltpu.make_async_remote_copy(
            src_ref=src, dst_ref=dst, send_sem=send, recv_sem=recv,
            device_id=device, device_id_type=MESH,
        )

    loads = [
        pltpu.make_async_copy(usable, flags_in, load_sem.at[0]),
        pltpu.make_async_copy(raw, band.at[pl.ds(HALO + zhi * BAND_ROWS, BAND_ROWS)], load_sem.at[1]),
    ]
    for load in loads:
        load.start()
    barrier = pltpu.get_barrier_semaphore()
    partners = [across] + [along_y(d) for d in (1, 3)]
    partners += [ahead(r) for r in (1, 2, 3, 4, 6, 8, -1, -2, -3, -4, -6, -8)]
    for partner in partners:
        pl.semaphore_signal(barrier, inc=1, device_id=partner, device_id_type=MESH)
    pl.semaphore_wait(barrier, len(partners))

    def z_copy(k):
        first, pairs = ACROSS[k]
        own = first + zhi * (PAIRS // 2 - 2 * first - pairs)
        return remote(
            raw.at[pl.ds(own * PAIR, pairs * PAIR)],
            band.at[pl.ds(HALO + zhi * BAND_ROWS + own * PAIR, pairs * PAIR)],
            z_send.at[k], z_recv.at[k], across,
        )

    z_copy(0).start()

    @pl.when(core == 0)
    def _():
        for k in range(1, len(ACROSS)):
            z_copy(k).start()

    loads[0].wait()
    once = flags_in[...].astype(jnp.float32)
    for g in range(5):
        flags[8 * g : 8 * g + 4, :] = once[4 * g : 4 * g + 4, :]
        flags[8 * g + 4 : 8 * g + 8, :] = once[4 * g : 4 * g + 4, :]
    flags[ROWS:FLAG_ROWS, :] = jnp.zeros((FLAG_ROWS - ROWS, CH), jnp.float32)
    white[0, 0:FLAG_ROWS, :] = flags[...].astype(jnp.bfloat16)
    for load in loads[1:]:
        load.wait()

    def halo_copy(top):
        src = GROUP_ROWS if top else HALO
        dst = 0 if top else HALO + GROUP_ROWS
        k = 0 if top else 1
        return remote(
            band.at[pl.ds(src, HALO)], band.at[pl.ds(dst, HALO)],
            h_send.at[k], h_recv.at[k], along_y(1 if top else 3),
        )

    def send_halo(own):
        pl.when(zhi == own)(halo_copy(True).start)
        pl.when(zhi != own)(halo_copy(False).start)

    flag_copies = [
        remote(
            white.at[0, pl.ds(0, FLAG_ROWS)], white.at[r, pl.ds(0, FLAG_ROWS)],
            f_send.at[r - 1], f_recv.at[r - 1], ahead(r),
        )
        for r in (1, 2, 3)
    ]

    sublane = lax.broadcasted_iota(jnp.int32, (1, 8, CH), 1)
    lane = lax.broadcasted_iota(jnp.int32, (1, 8, CH), 2)
    sign = jnp.where(sublane < 4, -1.0, 1.0)
    first_half = (lane % 32) < 16
    valid = flags[0:ROWS, :]

    def make_table():
        lag = lax.broadcasted_iota(jnp.int32, (LAG_PAD, STRIDE), 0)
        column = lax.broadcasted_iota(jnp.int32, (LAG_PAD, STRIDE), 1)
        bins = y * GROUP + jnp.where(column < GROUP, column, column - GROUP)
        lag_index = lag.astype(jnp.float32) - float(LAGS // 2)
        bin_freq = first_bin + bins.astype(jnp.float32)
        phase_angle = 2.0 * math.pi * lag_index * bin_freq / period
        both = jnp.where(column < GROUP, jnp.cos(phase_angle), -jnp.sin(phase_angle))
        table[...] = jnp.where(lag < LAGS, both, 0.0).astype(jnp.bfloat16)

    def magnitudes(row, pairs):
        def body(p):
            at = pl.multiple_of(row + p * PAIR, 16)
            v = band[pl.ds(at, PAIR), :].astype(jnp.float32).reshape(10, 8, CH)
            square = v * v
            m = jnp.sqrt(square + roll4(square))
            mag[pl.ds(at, PAIR), :] = m.reshape(PAIR, CH)

        loop(pairs, body)

    def whiten(start, pairs):
        def body(p):
            pair = start + p
            row = pl.multiple_of(pair * PAIR, 16)
            m = [mag[pl.ds(pl.multiple_of(row + t * ROWS, 8), ROWS), :] for t in range(10)]
            inner = ((m[1] + m[2]) + (m[3] + m[4])) + ((m[5] + m[6]) + (m[7] + m[8]))
            outs = []
            for t in range(2):
                bin_index = y * GROUP + 2 * pair + t
                count = (
                    jnp.minimum(bin_index + SMOOTH, BINS - 1) - jnp.maximum(bin_index - SMOOTH, 0) + 1
                ).astype(jnp.float32)
                total = inner + (m[0] if t == 0 else m[9])
                water = jnp.maximum(total / jnp.full((1, CH), count, jnp.float32), water_level)
                outs.append(valid / water)
            factor = jnp.concatenate(outs, axis=0)
            v = band[pl.ds(pl.multiple_of(row + HALO, 16), PAIR), :].astype(jnp.float32)
            w = (v * factor).astype(jnp.bfloat16)
            white[0, pl.ds(pl.multiple_of(FLAG_ROWS + row, 16), PAIR), :] = w
            a1 = pltpu.roll(w.astype(jnp.float32).reshape(10, 8, CH), 112 * zhi, axis=2)
            a2 = pltpu.roll(roll4(a1) * sign, 16, axis=2)
            both = jnp.where(first_half, a1, a2).reshape(PAIR, CH)
            turned = jnp.transpose(both)
            column = lax.broadcasted_iota(jnp.int32, (CH, PAIR), 1)
            lhs[pair, 0:CH, 0:PAIR] = jnp.where(column < ROWS, turned, 0.0).astype(jnp.bfloat16)
            lhs[pair, CH : 2 * CH, 0:PAIR] = jnp.where(column < ROWS, 0.0, turned).astype(jnp.bfloat16)

        loop(pairs, body)

    def cross(r, start, pairs):
        def body(p):
            pair = start + p
            rhs = white[r, pl.ds(pl.multiple_of(FLAG_ROWS + pair * PAIR, 16), PAIR), :]
            c = jnp.dot(lhs[pair, :, 0:PAIR], rhs, preferred_element_type=jnp.float32)
            for g in range(4):
                scale = inverse[r, g * 16 : (g + 1) * 16, :]
                for t in range(2):
                    for part in range(2):
                        at = t * CH + g * 32 + part * 16
                        row = g * 16 * STRIDE + part * GROUP + 2 * pair + t
                        spread[pl.ds(row, 16, stride=STRIDE), :] = c[at : at + 16, :] * scale

        loop(pairs, body)

    def usable_pairs(r):
        mine = white[0, 0:FLAG_ROWS, :].astype(jnp.float32)
        mine = pltpu.roll(mine, 112 * zhi, axis=1)
        n = jnp.dot(
            jnp.transpose(mine).astype(jnp.bfloat16), white[r, 0:FLAG_ROWS, :],
            preferred_element_type=jnp.float32,
        )
        scale = 1.0 / jnp.maximum(n * 0.5, 1.0)
        for g in range(4):
            inverse[r, g * 16 : (g + 1) * 16, :] = scale[g * 32 : g * 32 + 16, :]

    def lag_sums(r, to):
        tab = table[...]

        def body(p):
            a = OWN_ROWS * to + 2 * p
            s0 = spread[pl.ds(pl.multiple_of(a * STRIDE, 8), STRIDE), :].astype(jnp.bfloat16)
            s1 = spread[pl.ds(pl.multiple_of((a + 1) * STRIDE, 8), STRIDE), :].astype(jnp.bfloat16)
            both = jnp.concatenate([s0, s1], axis=1)
            c = jnp.dot(tab, both, preferred_element_type=jnp.float32)
            lagged[r, pl.ds(a, LAG_STORE, stride=HALF), :] = c[0:LAG_STORE, 0:CH]
            lagged[r, pl.ds(a + 1, LAG_STORE, stride=HALF), :] = c[0:LAG_STORE, CH : 2 * CH]

        loop(OWN_ROWS // 2, body)

    PARTS = ((2, 0, 1), (2, CUT, 3), (1, CUT, 1), (3, 0, 3), (1, 0, 1), (3, CUT, 3))

    def y_copy(r, n):
        d, row, way = PARTS[n]
        part = pl.ds(row, CUT if row == 0 else FULL - CUT)
        return remote(
            outbox.at[r, d - 1, part], inbox.at[r, d - 1, part], y_send.at[r, n], y_recv.at[r, n], along_y(way)
        )

    def pack_round(r, n):
        d, row, _ = PARTS[n]
        to = (y + d) % 4

        def body(l):
            at = pl.multiple_of(row + l * OWN_ROWS, 16)
            from_row = pl.multiple_of(row // OWN_ROWS * HALF + l * HALF + to * OWN_ROWS, 16)
            sums = lagged[r, pl.ds(from_row, OWN_ROWS), :]
            if n >= 4:
                sums = sums + inbox[r, 1, pl.ds(at, OWN_ROWS), :].astype(jnp.float32)
            outbox[r, d - 1, pl.ds(at, OWN_ROWS), :] = sums.astype(jnp.bfloat16)

        loop((CUT if row == 0 else FULL - CUT) // OWN_ROWS, body)

    def lags(r):
        lag_sums(r, (y + 2) % 4)
        for n in (0, 1):
            pack_round(r, n)
            y_copy(r, n).start()
        for n in (2, 3):
            lag_sums(r, (y + PARTS[n][0]) % 4)
            pack_round(r, n)
            y_copy(r, n).start()
        lag_sums(r, y)

    def relay(r):
        for n in (0, 1):
            y_copy(r, n).wait_recv()
            pack_round(r, 4 + n)
            y_copy(r, 4 + n).start()

    def total_round(r):
        def body(l):
            at = pl.multiple_of(l * OWN_ROWS, 16)
            sums = lagged[r, pl.ds(pl.multiple_of(l * HALF + y * OWN_ROWS, 16), OWN_ROWS), :]
            for d in (0, 2):
                sums = sums + inbox[r, d, pl.ds(at, OWN_ROWS), :].astype(jnp.float32)
            out[r, pl.ds(at, OWN_ROWS), :] = sums

        loop(LAGS, body)

    def finish(r):
        for n in (2, 3, 4, 5):
            y_copy(r, n).wait_recv()
        total_round(r)

    def piece(slot, k, origin):
        first, pairs = WHITEN[k]
        return white.at[slot, pl.ds(FLAG_ROWS + first_pair(first, pairs, origin) * PAIR, pairs * PAIR)]

    def to_sibling(k):
        return remote(piece(0, k, zhi), piece(1, k, zhi), x_send.at[0, k], x_recv.at[0, k], ahead(1))

    def to_next(k):
        return remote(piece(0, k, zhi), piece(2, k, zhi), x_send.at[1, k], x_recv.at[1, k], ahead(2))

    def pass_up(k):
        return remote(piece(2, k, before), piece(3, k, before), x_send.at[2, k], x_recv.at[2, k], ahead(1))

    def pass_down(k):
        return remote(piece(2, k, before), piece(1, k, before), x_send.at[2, k], x_recv.at[0, k], ahead(-1))

    def pass_on(k):
        return remote(piece(2, k, before), piece(3, k, before), x_send.at[0, k], x_recv.at[2, k], ahead(1))

    def detour_rows(k):
        first, pairs = WHITEN[k]
        return detour.at[pl.ds(first_pair(first, pairs, zhi) * PAIR, pairs * PAIR)]

    def detour_in(k, chips):
        return remote(piece(0, k, zhi), detour_rows(k), w_send.at[k], w_recv.at[k], ahead(-2 * chips))

    def detour_out(k, chips):
        return remote(detour_rows(k), piece(2, k, zhi), w_send.at[k], x_recv.at[1, k], ahead(2 + 2 * chips))

    last_chip = x_index == 3
    last_odd = last_chip & (core == 1)

    def helping(side, k):
        return (core == side) & (x_index == 3 - LEFT[side][k]) & (x_index != 3)

    def help_out(side, k):
        if LEFT[side][k]:
            @pl.when(helping(side, k))
            def _():
                detour_in(k, LEFT[side][k]).wait_recv()
                detour_out(k, LEFT[side][k]).start()

    def send_own(k):
        pl.when(core == 0)(to_sibling(k).start)
        pl.when(x_index != 3)(to_next(k).start)
        for side in (0, 1):
            chips = LEFT[side][k]
            pl.when(last_chip & (core == side))(detour_in(k, chips).start if chips else to_next(k).start)

    def go_on():
        pl.semaphore_signal(go_sem, inc=1, device_id=sibling, device_id_type=MESH)

    def forward(k):
        to_next(k).wait_recv()
        pl.when(core == 0)(pass_up(k).start)
        pl.when(core == 1)(pass_down(k).start)
        pl.when((core == 1) & (x_index != 3))(pass_on(k).start)

    def forward_early(k):
        @pl.when(x_index != 0)
        def _():
            forward(k)

    def whiten_piece(k):
        first, pairs = WHITEN[k]
        whiten(first_pair(first, pairs, zhi), pairs)
        send_own(k)

    def cross_piece(k):
        first, pairs = WHITEN[k]
        cross(0, first_pair(first, pairs, zhi), pairs)

    def receive_across(k):
        z_copy(k).wait_recv()
        if k == 0:
            send_halo(0)
        first, pairs = ACROSS[k]
        magnitudes(HALO + first_pair(first, pairs, 1 - zhi) * PAIR, pairs)

    send_halo(1)
    for copy in flag_copies:
        copy.start()
    magnitudes(HALO + zhi * BAND_ROWS, BAND // 2)
    whiten_piece(0)
    make_table()
    usable_pairs(0)
    receive_across(0)
    cross_piece(0)
    halo_copy(True).wait_recv()
    halo_copy(False).wait_recv()
    magnitudes(0, SMOOTH // 2)
    magnitudes(HALO + GROUP_ROWS, SMOOTH // 2)

    @pl.when(y == 0)
    def _():
        mag[0:HALO, :] = jnp.zeros((HALO, CH), jnp.float32)

    @pl.when(y == 3)
    def _():
        mag[HALO + GROUP_ROWS :, :] = jnp.zeros((HALO, CH), jnp.float32)

    whiten_piece(1)
    cross_piece(1)

    @pl.when(core == 1)
    def _():
        pl.semaphore_wait(go_sem, 1)
        for k in range(1, len(ACROSS)):
            z_copy(k).start()

    for k in range(2, PIECES):
        receive_across(k - 1)
        if k - 1 == TURN:
            pl.when(core == 0)(go_on)
        whiten_piece(k)
        forward_early(k - 2)
        help_out(0, k - 2)
        if k == 2:
            help_out(1, 0)
        if k == 4:
            pl.when(x_index == 0)(functools.partial(forward, 0))
        if k == 5:
            pl.when(last_odd)(pass_on(0).start)
        if k < PIECES - 1:
            cross_piece(k)
        if k == 3:
            for r in (1, 2, 3):
                flag_copies[r - 1].wait_recv()
                usable_pairs(r)

    for k in range(1, PIECES - 2):
        help_out(1, k)

    @pl.when(last_odd)
    def _():
        for k in range(1, PIECES - 2):
            pass_on(k).start()

    cross_piece(PIECES - 1)
    lags(0)
    for k in (PIECES - 2, PIECES - 1):
        forward_early(k)
        pl.when(last_odd)(pass_on(k).start)
        help_out(0, k)
        help_out(1, k)
    pl.when(core == 0)(lambda: relay(0))

    def forward_late(*pieces):
        for k in pieces:
            forward(k)

    def receive(slot):
        for k in range(PIECES):
            remote(
                piece(slot, k, zhi), piece(slot, k, zhi), x_send.at[0, k], x_recv.at[slot - 1, k], ahead(1)
            ).wait_recv()

    first_chip = x_index == 0
    second = 2 - core
    third = jnp.where(first_chip, 3, 1 + core)
    fourth = jnp.where(first_chip, 1 + core, 3)
    pl.when(first_chip & (core == 0))(lambda: forward_late(1, 2, 3, 4, 5))
    pl.when(core == 1)(lambda: receive(1))
    cross(second, 0, PAIRS)
    pl.when(first_chip & (core == 1))(lambda: forward_late(1, 2, 3))
    lags(second)
    pl.when(first_chip & (core == 1))(lambda: forward_late(4))
    relay(jnp.where(core == 0, second, 0))
    pl.when(first_chip)(lambda: receive(3))
    pl.when(jnp.logical_not(first_chip) & (core == 0))(lambda: receive(1))
    cross(third, 0, PAIRS)
    lags(third)
    pl.when(first_chip & (core == 1))(lambda: forward_late(5))
    pl.when(core == 1)(lambda: relay(1))
    pl.when(first_chip & (core == 0))(lambda: receive(1))
    pl.when(jnp.logical_not(first_chip))(lambda: receive(3))
    cross(fourth, 0, PAIRS)
    lags(fourth)
    relay(third)
    finish(0)
    finish(second)
    relay(fourth)
    finish(third)
    finish(fourth)

    for k in range(len(ACROSS)):
        z_copy(k).wait_send()
    halo_copy(True).wait_send()
    halo_copy(False).wait_send()
    for copy in flag_copies:
        copy.wait_send()
    for k in range(PIECES):
        detoured, helper = last_chip & (core == 2), core == 2
        for side in (0, 1):
            if LEFT[side][k]:
                detoured = detoured | (last_chip & (core == side))
                helper = helper | helping(side, k)
        pl.when(jnp.logical_not(detoured))(to_next(k).wait_send)
        pl.when(detoured | helper)(detour_in(k, 2).wait_send)
        to_sibling(k).wait_send()
        pass_up(k).wait_send()
    for r in range(ROUNDS):
        for n in range(len(PARTS)):
            y_copy(r, n).wait_send()


def on_device(spectra, valid):
    groups = spectra.reshape(5, 4, BAND, 2, CH)
    raw = jnp.transpose(groups, (2, 0, 3, 1, 4)).reshape(BAND_ROWS, CH)
    dma = pltpu.SemaphoreType.DMA
    bf16, f32 = jnp.bfloat16, jnp.float32
    out = pl.pallas_call(
        kernel,
        out_shape=jax.ShapeDtypeStruct((ROUNDS, LAGS * OWN_ROWS, CH), f32),
        in_specs=[pl.BlockSpec(memory_space=pl.ANY)] * 2,
        out_specs=pl.BlockSpec(memory_space=pltpu.VMEM),
        scratch_shapes=[
            pltpu.VMEM((GROUP_ROWS + 2 * HALO, CH), bf16),
            pltpu.VMEM((GROUP_ROWS + 2 * HALO, CH), f32),
            pltpu.VMEM((ROUNDS, FLAG_ROWS + GROUP_ROWS, CH), bf16),
            pltpu.VMEM((GROUP // 2, 2 * CH, CH), bf16),
            pltpu.VMEM((ROUNDS, HALF, CH), f32),
            pltpu.VMEM(((HALF + 1) * STRIDE, CH), f32),
            pltpu.VMEM((ROUNDS, (LAG_STORE + 1) * HALF, CH), f32),
            pltpu.VMEM((ROUNDS, 3, LAGS * OWN_ROWS, CH), bf16),
            pltpu.VMEM((ROUNDS, 3, LAGS * OWN_ROWS, CH), bf16),
            pltpu.VMEM((GROUP_ROWS, CH), bf16),
            pltpu.VMEM((W, CH), jnp.int32),
            pltpu.VMEM((FLAG_ROWS, CH), f32),
            pltpu.VMEM((LAG_PAD, STRIDE), bf16),
            dma((2,)), pltpu.SemaphoreType.REGULAR, dma((len(ACROSS),)), dma((len(ACROSS),)), dma((2,)), dma((2,)), dma((3,)), dma((3,)),
            dma((3, PIECES)), dma((3, PIECES)), dma((PIECES,)), dma((PIECES,)), dma((ROUNDS, 6)), dma((ROUNDS, 6)),
        ],
        compiler_params=pltpu.CompilerParams(
            collective_id=0, has_side_effects=True, vmem_limit_bytes=48 << 20
        ),
        name="correlate",
    )(raw, valid)
    return out.reshape(ROUNDS, 1, LAGS, OWN_ROWS, CH)


def solution(mesh):
    return jax.shard_map(
        on_device,
        mesh=mesh,
        in_specs=(P(None, "freq", None, "chan"), P(None, "chan")),
        out_specs=P(None, "chan", None, "freq", None),
        check_vma=False,
    )
```
